256 devices in a mesh: seg: 8 (over x, core), space: 32 (over z, y).
Axes of the slice: x: 4, y: 4, z: 8, core: 2. Of those that a mesh axis runs over, the one named last changes fastest.
Arguments:
- tangents: float32 [8, 25, 3, 128, 8, 128], P('seg', None, None, 'space'), may hold values from -700 to 700
- base_flow: float32 [8, 4, 3, 128, 8, 128], P('seg', None, None, 'space'), may hold values from -4 to 4
- viscosity: float32 [8, 128, 8, 128], P('seg', 'space'), may hold values from 0.02 to 0.2
- source: float32 [8, 3, 128, 8, 128], P('seg', None, 'space'), may hold values from -6 to 6
Outputs:
- handed: float32 [8, 25, 3, 128, 8, 128], P('seg', None, None, 'space')
- growth: float32 [8, 24], P('seg')
- projection: float32 [8, 24], P('seg')
The draws below stay inside these ranges and needn't reach their ends.
All inputs are finite; a program needn't handle non-finite values.
Results may differ from the reference program's by a relative error of at most 0.0003.
Values sent between devices are 32-bit elements; how exact they have to be, the bound alone decides.
A program may use at most 64 MiB of HBM per device.

```python
import math
import jax
import jax.numpy as jnp
from jax import lax

CY = 8
CZ = 128
STEPS = 4
TANG = 24
SEGS = 8
NX = 128


def draw_tangents(key, part):
    key = jax.random.fold_in(key, 11)
    noise_key = jax.random.fold_in(key, 0)
    scale_key = jax.random.fold_in(key, 2)
    shape = (SEGS, TANG + 1, 3, NX, CY, CZ)
    along_x = jnp.arange(NX, dtype=jnp.float32).reshape(1, 1, 1, NX, 1, 1)
    segment_rank = jnp.arange(SEGS, dtype=jnp.float32).reshape(SEGS, 1, 1, 1, 1, 1)
    noise = jnp.clip(jax.random.normal(noise_key, shape), -4.0, 4.0)
    mixed = noise + 0.6 * jnp.roll(noise, -1, axis=1) + 0.4 * jnp.roll(noise, -3, axis=1)
    tangent_scale = jnp.exp(jax.random.uniform(scale_key, (1, TANG + 1, 1, 1, 1, 1), minval=math.log(0.5), maxval=math.log(2.0)))
    rising = (1.0 + 2.0 * along_x / max(NX - 1, 1)) * (1.0 + 2.0 * segment_rank / max(SEGS - 1, 1))
    return (mixed * tangent_scale * rising).astype(jnp.float32)


def steps_of(stream_key, dims, shards, low, top_value):
    def one(axis_at, shards_of):
        heights = jax.random.uniform(jax.random.fold_in(jax.random.fold_in(stream_key, 6), axis_at), (shards_of,), jnp.float32, low / len(shards), top_value / len(shards))
        return jnp.repeat(jnp.exp(heights), dims[axis_at] // shards_of).reshape((-1,) + (1,) * (len(dims) - axis_at - 1))

    gain = one(*shards[0])
    for cut in shards[1:]:
        gain = gain * one(*cut)
    return gain


def centred(key, extent, deviation, most, cuts=(), kind=jnp.bfloat16):
    drawn = jax.random.normal(key, extent, jnp.float32) * deviation
    if len(cuts) > 0:
        drawn = steps_of(key, extent, cuts, -0.22, 0.18) * drawn
    return jnp.clip(drawn, min=-most, max=most).astype(kind)


def setup_inputs(seed: int = 0) -> dict:
    arg_keys = jax.random.split(jax.random.key(seed), 5)
    tangents = draw_tangents(jax.random.fold_in(arg_keys[4], 71), 0)
    base_flow = centred(arg_keys[1], (SEGS, STEPS, 3, NX, CY, CZ), 0.8, 4.0, ((0, 8), (3, 32)), jnp.float32)
    viscosity = jnp.clip(jnp.exp(math.log(0.2) - 2.3025851 * jax.random.uniform(arg_keys[2], (SEGS, NX, CY, CZ), jnp.float32) ** steps_of(arg_keys[2], (SEGS, NX, CY, CZ), ((0, 8), (1, 32)), -0.2, 0.2)), 0.02, 0.2)
    source = centred(arg_keys[3], (SEGS, 3, NX, CY, CZ), 1.0, 6.0, ((0, 8), (2, 32)), jnp.float32)
    return {"tangents": tangents, "base_flow": base_flow, "viscosity": viscosity, "source": source}


DT = 0.5

def pad_cross(tensor):
    widths = [(0, 0)] * (tensor.ndim - 2) + [(1, 1), (1, 1)]
    return jnp.pad(tensor, widths)

def neighbours(padded):
    centre = padded[..., 1:-1, 1:-1, 1:-1]
    neighbour_pairs = [(padded[..., 2:, 1:-1, 1:-1], padded[..., :-2, 1:-1, 1:-1]), (padded[..., 1:-1, 2:, 1:-1], padded[..., 1:-1, :-2, 1:-1]), (padded[..., 1:-1, 1:-1, 2:], padded[..., 1:-1, 1:-1, :-2])]
    return (centre, neighbour_pairs)

def advance(tangent_ext, flow_ext, viscous, forcing):
    centre, neighbour_pairs = neighbours(pad_cross(tangent_ext))
    flow_centre, flow_pairs = neighbours(pad_cross(flow_ext))
    transport = jnp.zeros_like(centre)
    product = jnp.zeros_like(centre)
    spread = -6.0 * centre
    for axis_number in range(3):
        forward, backward = neighbour_pairs[axis_number]
        flow_ahead, flow_behind = flow_pairs[axis_number]
        transport = transport + flow_centre[axis_number] * (0.5 * (forward - backward))
        flow_slope = 0.5 * (flow_ahead - flow_behind)
        product = product + centre[:, axis_number:axis_number + 1] * flow_slope[None]
        spread = spread + forward + backward
    tendency = -transport - product + viscous * spread
    updated = centre + DT * tendency
    driven = updated[-1:] + DT * forcing[None]
    return jnp.concatenate([updated[:-1], driven], axis=0)

def lower_cholesky(matrix):
    order = matrix.shape[0]
    places = jnp.arange(order)
    columns = []
    for column_index in range(order):
        accum = matrix[:, column_index]
        for earlier in range(column_index):
            accum = accum - columns[earlier] * columns[earlier][column_index]
        pivot = jnp.sqrt(accum[column_index])
        columns.append(jnp.where(places >= column_index, accum / pivot, jnp.zeros_like(accum)))
    return jnp.stack(columns, axis=1)

def lower_inverse(lower_factor):
    order = lower_factor.shape[0]
    identity_matrix = jnp.eye(order, dtype=lower_factor.dtype)
    rows = []
    for row_index in range(order):
        value = identity_matrix[row_index]
        if row_index > 0:
            value = value - jnp.dot(lower_factor[row_index, :row_index], jnp.stack(rows), precision=lax.Precision.HIGHEST)
        rows.append(value / lower_factor[row_index, row_index])
    return jnp.stack(rows)

def reference(tangents, base_flow, viscosity, source):
    cell_total = 3 * NX * CY * CZ
    handed_rows = [tangents[0]]
    growth_rows = []
    projection_rows = []
    running = jnp.zeros((TANG,), jnp.float32)
    for segment_index in range(SEGS):
        current = tangents[segment_index]
        for section_index in range(STEPS):
            extended = jnp.pad(current, ((0, 0), (0, 0), (1, 1), (0, 0), (0, 0)))
            flow_field = jnp.pad(base_flow[segment_index, section_index], ((0, 0), (1, 1), (0, 0), (0, 0)))
            current = advance(extended, flow_field, viscosity[segment_index], source[segment_index])
        flattened = current.reshape(TANG + 1, -1)
        homogeneous = flattened[:TANG]
        driven = flattened[TANG]
        gram_matrix = jnp.dot(homogeneous, homogeneous.T, precision=lax.Precision.HIGHEST) / cell_total
        lower_factor = lower_cholesky(gram_matrix)
        inverse_lower = lower_inverse(lower_factor)
        orthonormal = jnp.dot(inverse_lower, homogeneous, precision=lax.Precision.HIGHEST)
        projection = jnp.dot(orthonormal, driven, precision=lax.Precision.HIGHEST) / cell_total
        remainder = driven - jnp.dot(projection, orthonormal, precision=lax.Precision.HIGHEST)
        running = running + jnp.log(jnp.diagonal(lower_factor))
        growth_rows.append(running)
        projection_rows.append(projection)
        if segment_index + 1 < SEGS:
            handed_rows.append(jnp.concatenate([orthonormal, remainder[None]], axis=0).reshape(current.shape))
    return (jnp.stack(handed_rows), jnp.stack(growth_rows), jnp.stack(projection_rows))
```

```python
import functools

import jax
import jax.numpy as jnp
from jax import lax
from jax.experimental import pallas as pl
from jax.experimental.pallas import tpu as pltpu
from jax.sharding import PartitionSpec as P

MESH = pl.DeviceIdType.MESH
DT = 0.5
ROW = 4
SLAB = 4
WIDE = 3 * SLAB
STEPS = 4
AHEAD = 4


def signs(shape, dim):
    return lax.broadcasted_iota(jnp.int32, shape, dim)


def coefficients(s, flowx, viscx, srcx, coef, position, planes_total):
    lo, hi = s + 1, WIDE - 1 - s
    n = hi - lo
    first = position * SLAB - SLAB
    plane = first + lo - 1 + signs((n + 2, 8, 128), 0)
    inside = (plane >= 0) & (plane < planes_total)
    ahead_in, behind_in = inside[2:], inside[:n]
    rows, lanes = signs((n, 8, 128), 1), signs((n, 8, 128), 2)
    hn = DT * viscx[lo:hi]
    u = []
    for d in range(3):
        u.append(jnp.where(inside, flowx[s, d, lo - 1 : hi + 1], 0.0))
    hu = [(0.5 * DT) * u[d][1 : n + 1] for d in range(3)]
    coef[s, 0, lo:hi] = jnp.where(ahead_in, hn - hu[0], 0.0)
    coef[s, 1, lo:hi] = jnp.where(behind_in, hn + hu[0], 0.0)
    coef[s, 2, lo:hi] = jnp.where(rows < 7, hn - hu[1], 0.0)
    coef[s, 3, lo:hi] = jnp.where(rows > 0, hn + hu[1], 0.0)
    coef[s, 4, lo:hi] = jnp.where(lanes < 127, hn - hu[2], 0.0)
    coef[s, 5, lo:hi] = jnp.where(lanes > 0, hn + hu[2], 0.0)
    centre = 1.0 - 6.0 * hn
    for c in range(3):
        uc = u[c][1 : n + 1]
        slope = [
            u[c][2:] - u[c][:n],
            jnp.where(rows < 7, pltpu.roll(uc, 7, 1), 0.0)
            - jnp.where(rows > 0, pltpu.roll(uc, 1, 1), 0.0),
            jnp.where(lanes < 127, pltpu.roll(uc, 127, 2), 0.0)
            - jnp.where(lanes > 0, pltpu.roll(uc, 1, 2), 0.0),
        ]
        for d in range(3):
            local = (-0.5 * DT) * slope[d]
            if c == d:
                local = centre + local
            coef[s, 6 + 3 * c + d, lo:hi] = local


def step(s, src, dst, coef, base):
    lo, hi = s + 1, WIDE - 1 - s
    w = [src[c, lo:hi] for c in range(3)]
    k = [coef[s, i, lo:hi] for i in range(6)]
    for c in range(3):
        new = k[0] * src[c, lo + 1 : hi + 1] + k[1] * src[c, lo - 1 : hi - 1]
        new += k[2] * pltpu.roll(w[c], 7, 1) + k[3] * pltpu.roll(w[c], 1, 1)
        new += k[4] * pltpu.roll(w[c], 127, 2) + k[5] * pltpu.roll(w[c], 1, 2)
        for d in range(3):
            new += coef[s, 6 + 3 * c + d, lo:hi] * w[d]
        dst[c, lo - base : hi - base] = new


def eliminate(gram, count):
    rows, lanes = signs((32, 128), 0), signs((32, 128), 1)
    a = jnp.where(lanes == rows + 32, 1.0, gram)
    for j in range(count):
        row = a[j : j + 1, :]
        m = jnp.where(rows > j, a[:, j : j + 1] * (1.0 / a[j : j + 1, j : j + 1]), 0.0)
        a = a - m * row
    diagonal = jnp.where(lanes == rows, a, 0.0)
    pivots = jnp.sum(diagonal, axis=1, keepdims=True)
    scale = jnp.where(rows[:, :1] < count, 1.0 / jnp.sqrt(pivots), 1.0)
    return a, diagonal, scale


def kernel(
    sizes,
    tang, flow, visc, src,
    handed, growth, proj,
    ext, flowx, viscx, srcx, coef, tmp_a, tmp_b, stepped, prev, outv,
    accs, gram, spread, part_y, part_z, part_p, logs,
    local_sems, halo_send, halo_recv, side_send, side_recv,
    shift_send, shift_recv, y_send, y_recv, z_send, z_recv, p_send, p_recv,
    log_send, log_recv, out_sems,
):
    n_seg, n_space, count = sizes
    total = count + 1
    depth = n_space // ROW
    seg, pos = lax.axis_index("seg"), lax.axis_index("space")
    y, z = lax.rem(pos, ROW), pos // ROW
    right = (seg, lax.rem(pos + 1, n_space))
    left = (seg, lax.rem(pos + n_space - 1, n_space))

    def along_y(d):
        return (seg, z * ROW + lax.rem(y + d, ROW))

    def along_z(d, ds=0):
        return (lax.rem(seg + ds, n_seg), lax.rem(z + d, depth) * ROW + y)

    def along_seg(d):
        return (lax.rem(seg + d, n_seg), pos)

    senders = [left, right]
    senders += [along_y(d) for d in range(1, ROW)]
    senders += [along_z(d) for d in range(1, depth)]
    senders += [along_z(d, n_seg - 1) for d in range(1, depth)]
    senders += [along_seg(d) for d in range(1, n_seg)]
    barrier = pltpu.get_barrier_semaphore()
    for device in senders:
        pl.semaphore_signal(barrier, inc=1, device_id=device, device_id_type=MESH)

    own = pl.ds(SLAB, SLAB)
    locals_ = [
        pltpu.make_async_copy(tang.at[0], ext.at[:, :, own], local_sems.at[0]),
        pltpu.make_async_copy(flow.at[0], flowx.at[:, :, own], local_sems.at[1]),
        pltpu.make_async_copy(visc.at[0], viscx.at[own], local_sems.at[2]),
        pltpu.make_async_copy(src.at[0], srcx.at[:, own], local_sems.at[3]),
    ]
    for copy in locals_:
        copy.start()
    stepped[...] = jnp.zeros_like(stepped)
    gram[...] = jnp.zeros_like(gram)

    def remote(a, b, send, recv, device):
        return pltpu.make_async_remote_copy(
            src_ref=a, dst_ref=b, send_sem=send, recv_sem=recv,
            device_id=device, device_id_type=MESH,
        )

    def halo(k):
        return [
            remote(tang.at[0, k], ext.at[k, :, pl.ds(0, SLAB)],
                   halo_send.at[0, k], halo_recv.at[0, k], right),
            remote(tang.at[0, k], ext.at[k, :, pl.ds(2 * SLAB, SLAB)],
                   halo_send.at[1, k], halo_recv.at[1, k], left),
        ]

    sides = []
    for s in range(STEPS):
        n = SLAB - s
        sides.append(remote(flow.at[0, s, :, pl.ds(s, n)], flowx.at[s, :, pl.ds(s, n)],
                            side_send.at[0, s], side_recv.at[0, s], right))
        sides.append(remote(flow.at[0, s, :, pl.ds(0, n)], flowx.at[s, :, pl.ds(2 * SLAB, n)],
                            side_send.at[1, s], side_recv.at[1, s], left))
    n = SLAB - 1
    sides.append(remote(visc.at[0, pl.ds(1, n)], viscx.at[pl.ds(1, n)],
                        side_send.at[0, 4], side_recv.at[0, 4], right))
    sides.append(remote(visc.at[0, pl.ds(0, n)], viscx.at[pl.ds(2 * SLAB, n)],
                        side_send.at[1, 4], side_recv.at[1, 4], left))
    sides.append(remote(src.at[0, :, pl.ds(1, n)], srcx.at[:, pl.ds(1, n)],
                        side_send.at[0, 5], side_recv.at[0, 5], right))
    sides.append(remote(src.at[0, :, pl.ds(0, n)], srcx.at[:, pl.ds(2 * SLAB, n)],
                        side_send.at[1, 5], side_recv.at[1, 5], left))

    pl.semaphore_wait(barrier, len(senders))
    for copy in sides:
        copy.start()
    for k in range(AHEAD):
        for copy in halo(k):
            copy.start()
    for copy in locals_:
        copy.wait()
    for copy in sides:
        copy.wait_recv()
    for s in range(STEPS):
        coefficients(s, flowx, viscx, srcx, coef, pos, n_space * SLAB)

    def shift(k):
        return remote(stepped.at[k], prev.at[k], shift_send.at[k], shift_recv.at[k], along_seg(1))

    rows, lanes = signs((32, 128), 0), signs((32, 128), 1)

    def one(k, carry):
        for copy in halo(k):
            copy.wait_recv()

        @pl.when(k + AHEAD < total)
        def _():
            for copy in halo(k + AHEAD):
                copy.start()

        chain = [ext.at[k], tmp_a, tmp_b, tmp_a, stepped.at[k]]
        for s in range(STEPS):
            final = s == STEPS - 1
            step(s, chain[s], chain[s + 1], coef, SLAB if final else 0)

            @pl.when(k == count)
            def _():
                lo, hi = s + 1, WIDE - 1 - s
                base = SLAB if final else 0
                dst = chain[s + 1]
                for c in range(3):
                    dst[c, lo - base : hi - base] = dst[c, lo - base : hi - base] + DT * srcx[c, lo:hi]

        shift(k).start()
        w = stepped[k]
        for j in range(total):
            accs[8 * j : 8 * j + 8, :] = jnp.sum(w * stepped[j], axis=(0, 1))
        folded = accs[pl.ds(0, 32, stride=8), :]
        for i in range(1, 8):
            folded += accs[pl.ds(i, 32, stride=8), :]
        column = jnp.sum(folded, axis=1, keepdims=True)
        row = jnp.sum(jnp.where(rows == lanes, column, 0.0), axis=0, keepdims=True)
        g = gram[...]
        g = jnp.where((lanes == k) & (rows <= k), column, g)
        g = jnp.where((rows == k) & (lanes <= k), row, g)
        gram[...] = g
        return carry

    accs[8 * total :, :] = jnp.zeros((8 * (32 - total), 128), jnp.float32)
    lax.fori_loop(0, total, one, 0)

    cells = 3 * SLAB * 8 * 128 * n_space
    packed = gram[0:8, :]
    for i in range(1, 4):
        packed += pltpu.roll(gram[8 * i : 8 * i + 8, :], 32 * i, 1)
    part_y[y] = packed * (1.0 / cells)

    def exchange_y(d):
        return remote(part_y.at[y], part_y.at[y], y_send.at[d], y_recv.at[y], along_y(d))

    def exchange_z(d):
        return remote(part_z.at[z], part_z.at[z], z_send.at[d], z_recv.at[z], along_z(d))

    def exchange_p(d):
        return remote(part_z.at[z], part_p.at[z], p_send.at[d], p_recv.at[z], along_z(d, 1))

    def arrived(slot, sems, position):
        remote(slot.at[position], slot.at[position], y_send.at[0], sems.at[position], left).wait_recv()

    for d in range(1, ROW):
        exchange_y(d).start()
    for d in range(1, ROW):
        arrived(part_y, y_recv, lax.rem(y + d, ROW))
    part_z[z] = part_y[0] + part_y[1] + part_y[2] + part_y[3]
    for d in range(1, depth):
        exchange_z(d).start()
    for d in range(depth):
        exchange_p(d).start()
    for d in range(1, depth):
        arrived(part_z, z_recv, lax.rem(z + d, depth))
    for d in range(depth):
        arrived(part_p, p_recv, lax.rem(z + d, depth))

    def unpack(slots):
        sums = slots[0]
        for i in range(1, depth):
            sums = sums + slots[i]
        narrow = signs((8, 128), 1) < 32
        pieces = [jnp.where(narrow, sums, 0.0)]
        for i in range(1, 4):
            pieces.append(jnp.where(narrow, pltpu.roll(sums, 128 - 32 * i, 1), 0.0))
        return jnp.concatenate(pieces, axis=0)

    before, _, scale = eliminate(unpack(part_p), count)
    weights = before * scale
    for k in range(total):
        spread[k] = jnp.broadcast_to(weights[:, 32 + k : 33 + k], (32, 128))

    mine, diagonal, my_scale = eliminate(unpack(part_z), count)
    lane = signs((8, 128), 1)
    pivot_row = jnp.broadcast_to(jnp.sum(diagonal, axis=0, keepdims=True), (8, 128))
    logs[seg] = 0.5 * jnp.log(jnp.where(lane < count, pivot_row, 1.0))

    def exchange_log(d):
        return remote(logs.at[seg], logs.at[seg], log_send.at[d], log_recv.at[seg], along_seg(d))

    for d in range(1, n_seg):
        exchange_log(d).start()
    inner = jnp.where(rows == lanes, mine[:, count : count + 1] * my_scale, 0.0)
    proj[...] = jnp.sum(inner, axis=0, keepdims=True)[:, :count]

    for k in range(total):
        shift(k).wait_recv()

    @pl.when(seg == 0)
    def _():
        copy = pltpu.make_async_copy(tang, handed, out_sems.at[0])
        copy.start()
        copy.wait()

    @pl.when(seg > 0)
    def _():
        def combine(i, carry):
            c, x = i // SLAB, lax.rem(i, SLAB)
            w = [prev[k, c, x] for k in range(total)]
            for j in range(total):
                new = jnp.broadcast_to(spread[0, j : j + 1, :], (8, 128)) * w[0]
                for k in range(1, j + 1):
                    new += jnp.broadcast_to(spread[k, j : j + 1, :], (8, 128)) * w[k]
                outv[j, c, x] = new
            return carry

        def out(c):
            return pltpu.make_async_copy(outv.at[:, c], handed.at[0, :, c], out_sems.at[c])

        for c in range(3):
            lax.fori_loop(c * SLAB, (c + 1) * SLAB, combine, 0)
            out(c).start()
        for c in range(3):
            out(c).wait()

    for d in range(1, n_seg):
        arrived(logs, log_recv, lax.rem(seg + d, n_seg))
    sums = jnp.zeros((8, 128), jnp.float32)
    for i in range(n_seg):
        sums = sums + jnp.where(i <= seg, logs[i], 0.0)
    growth[...] = sums[0:1, :count]

    for copy in sides:
        copy.wait_send()

    def left_here(k, carry):
        for copy in halo(k):
            copy.wait_send()
        shift(k).wait_send()
        return carry

    lax.fori_loop(0, total, left_here, 0)
    for d in range(1, ROW):
        exchange_y(d).wait_send()
    for d in range(1, depth):
        exchange_z(d).wait_send()
    for d in range(depth):
        exchange_p(d).wait_send()
    for d in range(1, n_seg):
        exchange_log(d).wait_send()


def body(tangents, base_flow, viscosity, source):
    n_seg, n_space = lax.axis_size("seg"), lax.axis_size("space")
    total = tangents.shape[1]
    count = total - 1
    depth = n_space // ROW
    f32 = jnp.float32
    field = (3, SLAB, 8, 128)
    dma = pltpu.SemaphoreType.DMA
    any_spec = pl.BlockSpec(memory_space=pl.ANY)
    vmem_spec = pl.BlockSpec(memory_space=pltpu.VMEM)
    return pl.pallas_call(
        functools.partial(kernel, (n_seg, n_space, count)),
        out_shape=(
            jax.ShapeDtypeStruct(tangents.shape, f32),
            jax.ShapeDtypeStruct((1, count), f32),
            jax.ShapeDtypeStruct((1, count), f32),
        ),
        in_specs=[any_spec] * 4,
        out_specs=(any_spec, vmem_spec, vmem_spec),
        scratch_shapes=[
            pltpu.VMEM((total, 3, WIDE, 8, 128), f32),
            pltpu.VMEM((STEPS, 3, WIDE, 8, 128), f32),
            pltpu.VMEM((WIDE, 8, 128), f32),
            pltpu.VMEM((3, WIDE, 8, 128), f32),
            pltpu.VMEM((STEPS, 15, WIDE, 8, 128), f32),
            pltpu.VMEM((3, WIDE, 8, 128), f32),
            pltpu.VMEM((3, WIDE, 8, 128), f32),
            pltpu.VMEM((total,) + field, f32),
            pltpu.VMEM((total,) + field, f32),
            pltpu.VMEM((total,) + field, f32),
            pltpu.VMEM((256, 128), f32),
            pltpu.VMEM((32, 128), f32),
            pltpu.VMEM((total, 32, 128), f32),
            pltpu.VMEM((ROW, 8, 128), f32),
            pltpu.VMEM((depth, 8, 128), f32),
            pltpu.VMEM((depth, 8, 128), f32),
            pltpu.VMEM((n_seg, 8, 128), f32),
            dma((4,)),
            dma((2, total)),
            dma((2, total)),
            dma((2, 6)),
            dma((2, 6)),
            dma((total,)),
            dma((total,)),
            dma((ROW,)),
            dma((ROW,)),
            dma((depth,)),
            dma((depth,)),
            dma((depth,)),
            dma((depth,)),
            dma((n_seg,)),
            dma((n_seg,)),
            dma((3,)),
        ],
        compiler_params=pltpu.CompilerParams(
            collective_id=0, has_side_effects=True, vmem_limit_bytes=40 * 1024 * 1024
        ),
    )(tangents, base_flow, viscosity, source)


def solution(mesh):
    return jax.shard_map(
        body,
        mesh=mesh,
        in_specs=(
            P("seg", None, None, "space", None, None),
            P("seg", None, None, "space", None, None),
            P("seg", "space", None, None),
            P("seg", None, "space", None, None),
        ),
        out_specs=(P("seg", None, None, "space", None, None), P("seg", None), P("seg", None)),
        check_vma=False,
    )
```

```python
import functools

import jax
import jax.numpy as jnp
from jax import lax
from jax.experimental import pallas as pl
from jax.experimental.pallas import tpu as pltpu
from jax.sharding import PartitionSpec as P

MESH = pl.DeviceIdType.MESH
DT = 0.5
ROW = 4
SLAB = 4
WIDE = 3 * SLAB
STEPS = 4
AHEAD = 8


def signs(shape, dim):
    return lax.broadcasted_iota(jnp.int32, shape, dim)


def coefficients(s, flowx, viscx, srcx, coef, position, planes_total):
    lo, hi = s + 1, WIDE - 1 - s
    n = hi - lo
    first = position * SLAB - SLAB
    plane = first + lo - 1 + signs((n + 2, 8, 128), 0)
    inside = (plane >= 0) & (plane < planes_total)
    ahead_in, behind_in = inside[2:], inside[:n]
    rows, lanes = signs((n, 8, 128), 1), signs((n, 8, 128), 2)
    hn = DT * viscx[lo:hi]
    u = []
    for d in range(3):
        u.append(jnp.where(inside, flowx[s, d, lo - 1 : hi + 1], 0.0))
    hu = [(0.5 * DT) * u[d][1 : n + 1] for d in range(3)]
    coef[s, 0, lo:hi] = jnp.where(ahead_in, hn - hu[0], 0.0)
    coef[s, 1, lo:hi] = jnp.where(behind_in, hn + hu[0], 0.0)
    coef[s, 2, lo:hi] = jnp.where(rows < 7, hn - hu[1], 0.0)
    coef[s, 3, lo:hi] = jnp.where(rows > 0, hn + hu[1], 0.0)
    coef[s, 4, lo:hi] = jnp.where(lanes < 127, hn - hu[2], 0.0)
    coef[s, 5, lo:hi] = jnp.where(lanes > 0, hn + hu[2], 0.0)
    centre = 1.0 - 6.0 * hn
    for c in range(3):
        uc = u[c][1 : n + 1]
        slope = [
            u[c][2:] - u[c][:n],
            jnp.where(rows < 7, pltpu.roll(uc, 7, 1), 0.0)
            - jnp.where(rows > 0, pltpu.roll(uc, 1, 1), 0.0),
            jnp.where(lanes < 127, pltpu.roll(uc, 127, 2), 0.0)
            - jnp.where(lanes > 0, pltpu.roll(uc, 1, 2), 0.0),
        ]
        for d in range(3):
            local = (-0.5 * DT) * slope[d]
            if c == d:
                local = centre + local
            coef[s, 6 + 3 * c + d, lo:hi] = local


def step(s, src, dst, coef, base):
    lo, hi = s + 1, WIDE - 1 - s
    w = [src[c, lo:hi] for c in range(3)]
    k = [coef[s, i, lo:hi] for i in range(6)]
    for c in range(3):
        new = k[0] * src[c, lo + 1 : hi + 1] + k[1] * src[c, lo - 1 : hi - 1]
        new += k[2] * pltpu.roll(w[c], 7, 1) + k[3] * pltpu.roll(w[c], 1, 1)
        new += k[4] * pltpu.roll(w[c], 127, 2) + k[5] * pltpu.roll(w[c], 1, 2)
        for d in range(3):
            new += coef[s, 6 + 3 * c + d, lo:hi] * w[d]
        dst[c, lo - base : hi - base] = new


def eliminate(gram, count):
    rows, lanes = signs((32, 128), 0), signs((32, 128), 1)
    a = jnp.where(lanes == rows + 32, 1.0, gram)
    for j in range(count):
        row = a[j : j + 1, :]
        m = jnp.where(rows > j, a[:, j : j + 1] * (1.0 / a[j : j + 1, j : j + 1]), 0.0)
        a = a - m * row
    diagonal = jnp.where(lanes == rows, a, 0.0)
    pivots = jnp.sum(diagonal, axis=1, keepdims=True)
    scale = jnp.where(rows[:, :1] < count, 1.0 / jnp.sqrt(pivots), 1.0)
    return a, diagonal, scale


def kernel(
    sizes,
    tang, flow, visc, src,
    handed, growth, proj,
    ext, flowx, viscx, srcx, coef, tmp_a, tmp_b, stepped, prev,
    accs, gram, spread, weights, received, part_y, part_z, logs,
    local_sems, halo_send, halo_recv, side_send, side_recv,
    shift_send, shift_recv, y_send, y_recv, z_send, z_recv,
    log_send, log_recv, weight_sems, rounds,
):
    n_seg, n_space, count = sizes
    total = count + 1
    depth = n_space // ROW
    seg, pos = lax.axis_index("seg"), lax.axis_index("space")
    y, z = lax.rem(pos, ROW), pos // ROW
    right = (seg, lax.rem(pos + 1, n_space))
    left = (seg, lax.rem(pos + n_space - 1, n_space))

    def along_y(d):
        return (seg, z * ROW + lax.rem(y + d, ROW))

    def along_z(d, ds=0):
        return (lax.rem(seg + ds, n_seg), lax.rem(z + d, depth) * ROW + y)

    def along_seg(d):
        return (lax.rem(seg + d, n_seg), pos)

    near = [along_y(1), along_y(ROW - 1), along_z(1), along_z(depth - 1)]
    near += [along_seg(d % n_seg) for d in (1, -1, 2, -2)]
    greeted = [right, left] + near

    def greet(sem, devices):
        for device in devices:
            pl.semaphore_signal(sem, inc=1, device_id=device, device_id_type=MESH)

    barrier = pltpu.get_barrier_semaphore()
    greet(barrier, greeted)

    own = pl.ds(SLAB, SLAB)
    locals_ = [
        pltpu.make_async_copy(tang.at[0], ext.at[:, :, own], local_sems.at[0]),
        pltpu.make_async_copy(flow.at[0], flowx.at[:, :, own], local_sems.at[1]),
        pltpu.make_async_copy(visc.at[0], viscx.at[own], local_sems.at[2]),
        pltpu.make_async_copy(src.at[0], srcx.at[:, own], local_sems.at[3]),
    ]
    for copy in locals_:
        copy.start()
    stepped[...] = jnp.zeros_like(stepped)
    gram[...] = jnp.zeros_like(gram)

    def remote(a, b, send, recv, device):
        return pltpu.make_async_remote_copy(
            src_ref=a, dst_ref=b, send_sem=send, recv_sem=recv,
            device_id=device, device_id_type=MESH,
        )

    def halo(k):
        return [
            remote(tang.at[0, k], ext.at[k, :, pl.ds(0, SLAB)],
                   halo_send.at[0, k], halo_recv.at[0, k], right),
            remote(tang.at[0, k], ext.at[k, :, pl.ds(2 * SLAB, SLAB)],
                   halo_send.at[1, k], halo_recv.at[1, k], left),
        ]

    sides = []
    for s in range(STEPS):
        n = SLAB - s
        sides.append(remote(flow.at[0, s, :, pl.ds(s, n)], flowx.at[s, :, pl.ds(s, n)],
                            side_send.at[0, s], side_recv.at[0, s], right))
        sides.append(remote(flow.at[0, s, :, pl.ds(0, n)], flowx.at[s, :, pl.ds(2 * SLAB, n)],
                            side_send.at[1, s], side_recv.at[1, s], left))
    n = SLAB - 1
    sides.append(remote(visc.at[0, pl.ds(1, n)], viscx.at[pl.ds(1, n)],
                        side_send.at[0, 4], side_recv.at[0, 4], right))
    sides.append(remote(visc.at[0, pl.ds(0, n)], viscx.at[pl.ds(2 * SLAB, n)],
                        side_send.at[1, 4], side_recv.at[1, 4], left))
    sides.append(remote(src.at[0, :, pl.ds(1, n)], srcx.at[:, pl.ds(1, n)],
                        side_send.at[0, 5], side_recv.at[0, 5], right))
    sides.append(remote(src.at[0, :, pl.ds(0, n)], srcx.at[:, pl.ds(2 * SLAB, n)],
                        side_send.at[1, 5], side_recv.at[1, 5], left))

    pl.semaphore_wait(barrier, len(greeted))
    for copy in sides:
        copy.start()
    for k in range(min(AHEAD, total)):
        for copy in halo(k):
            copy.start()
    greet(rounds.at[0], near)
    for copy in locals_:
        copy.wait()
    for copy in sides:
        copy.wait_recv()
    for s in range(STEPS):
        coefficients(s, flowx, viscx, srcx, coef, pos, n_space * SLAB)

    def shift(k):
        return remote(stepped.at[k], prev.at[k], shift_send.at[k], shift_recv.at[k], along_seg(1))

    rows, lanes = signs((32, 128), 0), signs((32, 128), 1)

    def one(k, carry):
        for copy in halo(k):
            copy.wait_recv()

        @pl.when(k + AHEAD < total)
        def _():
            for copy in halo(k + AHEAD):
                copy.start()

        @pl.when(k == 2)
        def _():
            pl.semaphore_wait(rounds.at[0], len(near))
            greet(rounds.at[1], near[2:4])

        @pl.when(k == 4)
        def _():
            pl.semaphore_wait(rounds.at[1], 2)
            greet(rounds.at[2], near[2:4])

        @pl.when(k == 6)
        def _():
            pl.semaphore_wait(rounds.at[2], 2)

        chain = [ext.at[k], tmp_a, tmp_b, tmp_a, stepped.at[k]]
        for s in range(STEPS):
            final = s == STEPS - 1
            step(s, chain[s], chain[s + 1], coef, SLAB if final else 0)

            @pl.when(k == count)
            def _():
                lo, hi = s + 1, WIDE - 1 - s
                base = SLAB if final else 0
                dst = chain[s + 1]
                for c in range(3):
                    dst[c, lo - base : hi - base] = dst[c, lo - base : hi - base] + DT * srcx[c, lo:hi]

        shift(k).start()
        w = stepped[k]
        for j in range(total):
            accs[8 * j : 8 * j + 8, :] = jnp.sum(w * stepped[j], axis=(0, 1))
        folded = accs[pl.ds(0, 32, stride=8), :]
        for i in range(1, 8):
            folded += accs[pl.ds(i, 32, stride=8), :]
        column = jnp.sum(folded, axis=1, keepdims=True)
        row = jnp.sum(jnp.where(rows == lanes, column, 0.0), axis=0, keepdims=True)
        g = gram[...]
        g = jnp.where((lanes == k) & (rows <= k), column, g)
        g = jnp.where((rows == k) & (lanes <= k), row, g)
        gram[...] = g
        return carry

    accs[8 * total :, :] = jnp.zeros((8 * (32 - total), 128), jnp.float32)
    lax.fori_loop(0, total, one, 0)

    cells = 3 * SLAB * 8 * 128 * n_space
    packed = gram[0:8, :]
    for i in range(1, 4):
        packed += pltpu.roll(gram[8 * i : 8 * i + 8, :], 32 * i, 1)
    part_y[y] = packed * (1.0 / cells)

    def exchange_y(d):
        return remote(part_y.at[y], part_y.at[y], y_send.at[d], y_recv.at[y], along_y(d))

    def exchange_z(d):
        return remote(part_z.at[z], part_z.at[z], z_send.at[d], z_recv.at[z], along_z(d))

    def arrived(slot, sems, position):
        remote(slot.at[position], slot.at[position], y_send.at[0], sems.at[position], left).wait_recv()

    for d in range(1, ROW):
        exchange_y(d).start()
    for d in range(1, ROW):
        arrived(part_y, y_recv, lax.rem(y + d, ROW))
    part_z[z] = part_y[0] + part_y[1] + part_y[2] + part_y[3]
    for d in range(1, depth):
        exchange_z(d).start()
    for d in range(1, depth):
        arrived(part_z, z_recv, lax.rem(z + d, depth))

    def unpack(slots):
        sums = slots[0]
        for i in range(1, depth):
            sums = sums + slots[i]
        narrow = signs((8, 128), 1) < 32
        pieces = [jnp.where(narrow, sums, 0.0)]
        for i in range(1, 4):
            pieces.append(jnp.where(narrow, pltpu.roll(sums, 128 - 32 * i, 1), 0.0))
        return jnp.concatenate(pieces, axis=0)

    mine, diagonal, scale = eliminate(unpack(part_z), count)
    weights[...] = mine * scale
    hand_on = remote(weights, received, weight_sems.at[0], weight_sems.at[1], along_seg(1))
    hand_on.start()
    lane = signs((8, 128), 1)
    pivot_row = jnp.broadcast_to(jnp.sum(diagonal, axis=0, keepdims=True), (8, 128))
    logs[seg] = 0.5 * jnp.log(jnp.where(lane < count, pivot_row, 1.0))

    def exchange_log(d):
        return remote(logs.at[seg], logs.at[seg], log_send.at[d], log_recv.at[seg], along_seg(d))

    for d in range(1, n_seg):
        exchange_log(d).start()
    inner = jnp.where(rows == lanes, mine[:, count : count + 1] * scale, 0.0)
    proj[...] = jnp.sum(inner, axis=0, keepdims=True)[:, :count]

    for k in range(total):
        shift(k).wait_recv()
    hand_on.wait_recv()

    @pl.when(seg == 0)
    def _():
        def keep(k, carry):
            handed[k] = ext[k, :, SLAB : 2 * SLAB]
            return carry

        lax.fori_loop(0, total, keep, 0)

    @pl.when(seg > 0)
    def _():
        for k in range(total):
            spread[k] = jnp.broadcast_to(received[:, 32 + k : 33 + k], (32, 128))

        def combine(i, carry):
            c, x = i // SLAB, lax.rem(i, SLAB)
            w = [prev[k, c, x] for k in range(total)]
            for j in range(total):
                new = jnp.broadcast_to(spread[0, j : j + 1, :], (8, 128)) * w[0]
                for k in range(1, j + 1):
                    new += jnp.broadcast_to(spread[k, j : j + 1, :], (8, 128)) * w[k]
                handed[j, c, x] = new
            return carry

        lax.fori_loop(0, 3 * SLAB, combine, 0)

    for d in range(1, n_seg):
        arrived(logs, log_recv, lax.rem(seg + d, n_seg))
    sums = jnp.zeros((8, 128), jnp.float32)
    for i in range(n_seg):
        sums = sums + jnp.where(i <= seg, logs[i], 0.0)
    growth[...] = sums[0:1, :count]

    for copy in sides:
        copy.wait_send()

    def left_here(k, carry):
        for copy in halo(k):
            copy.wait_send()
        shift(k).wait_send()
        return carry

    lax.fori_loop(0, total, left_here, 0)
    for d in range(1, ROW):
        exchange_y(d).wait_send()
    for d in range(1, depth):
        exchange_z(d).wait_send()
    for d in range(1, n_seg):
        exchange_log(d).wait_send()
    hand_on.wait_send()


def body(tangents, base_flow, viscosity, source):
    n_seg, n_space = lax.axis_size("seg"), lax.axis_size("space")
    total = tangents.shape[1]
    count = total - 1
    depth = n_space // ROW
    f32 = jnp.float32
    field = (3, SLAB, 8, 128)
    dma = pltpu.SemaphoreType.DMA
    any_spec = pl.BlockSpec(memory_space=pl.ANY)
    vmem_spec = pl.BlockSpec(memory_space=pltpu.VMEM)
    inputs = [
        pltpu.with_memory_space_constraint(x, pltpu.HBM)
        for x in (tangents, base_flow, viscosity, source)
    ]
    handed, growth, proj = pl.pallas_call(
        functools.partial(kernel, (n_seg, n_space, count)),
        out_shape=(
            jax.ShapeDtypeStruct((total,) + field, f32),
            jax.ShapeDtypeStruct((1, count), f32),
            jax.ShapeDtypeStruct((1, count), f32),
        ),
        in_specs=[any_spec] * 4,
        out_specs=(vmem_spec,) * 3,
        scratch_shapes=[
            pltpu.VMEM((total, 3, WIDE, 8, 128), f32),
            pltpu.VMEM((STEPS, 3, WIDE, 8, 128), f32),
            pltpu.VMEM((WIDE, 8, 128), f32),
            pltpu.VMEM((3, WIDE, 8, 128), f32),
            pltpu.VMEM((STEPS, 15, WIDE, 8, 128), f32),
            pltpu.VMEM((3, WIDE, 8, 128), f32),
            pltpu.VMEM((3, WIDE, 8, 128), f32),
            pltpu.VMEM((total,) + field, f32),
            pltpu.VMEM((total,) + field, f32),
            pltpu.VMEM((256, 128), f32),
            pltpu.VMEM((32, 128), f32),
            pltpu.VMEM((total, 32, 128), f32),
            pltpu.VMEM((32, 128), f32),
            pltpu.VMEM((32, 128), f32),
            pltpu.VMEM((ROW, 8, 128), f32),
            pltpu.VMEM((depth, 8, 128), f32),
            pltpu.VMEM((n_seg, 8, 128), f32),
            dma((4,)),
            dma((2, total)),
            dma((2, total)),
            dma((2, 6)),
            dma((2, 6)),
            dma((total,)),
            dma((total,)),
            dma((ROW,)),
            dma((ROW,)),
            dma((depth,)),
            dma((depth,)),
            dma((n_seg,)),
            dma((n_seg,)),
            dma((2,)),
            pltpu.SemaphoreType.REGULAR((3,)),
        ],
        compiler_params=pltpu.CompilerParams(
            collective_id=0, has_side_effects=True, vmem_limit_bytes=32 * 1024 * 1024
        ),
    )(*inputs)
    return (handed[None], growth, proj)


def solution(mesh):
    return jax.shard_map(
        body,
        mesh=mesh,
        in_specs=(
            P("seg", None, None, "space", None, None),
            P("seg", None, None, "space", None, None),
            P("seg", "space", None, None),
            P("seg", None, "space", None, None),
        ),
        out_specs=(P("seg", None, None, "space", None, None), P("seg", None), P("seg", None)),
        check_vma=False,
    )
```

```python
import functools

import jax
import jax.numpy as jnp
from jax import lax
from jax.experimental import pallas as pl
from jax.experimental.pallas import tpu as pltpu
from jax.sharding import PartitionSpec as P

MESH = pl.DeviceIdType.MESH
DT = 0.5
ROW = 4
SLAB = 4
HALO = 2
WIDE = SLAB + 2 * HALO
STEPS = 4
AHEAD = 12
LAG = 12


def signs(shape, dim):
    return lax.broadcasted_iota(jnp.int32, shape, dim)


def span(s):
    edge = 1 + s % HALO
    return edge, WIDE - edge


def coefficients(s, flowx, viscx, srcx, coef, position, planes_total):
    lo, hi = span(s)
    n = hi - lo
    first = position * SLAB - HALO
    plane = first + lo - 1 + signs((n + 2, 8, 128), 0)
    inside = (plane >= 0) & (plane < planes_total)
    ahead_in, behind_in = inside[2:], inside[:n]
    rows, lanes = signs((n, 8, 128), 1), signs((n, 8, 128), 2)
    hn = DT * viscx[lo:hi]
    u = []
    for d in range(3):
        u.append(jnp.where(inside, flowx[s, d, lo - 1 : hi + 1], 0.0))
    hu = [(0.5 * DT) * u[d][1 : n + 1] for d in range(3)]
    coef[s, 0, lo:hi] = jnp.where(ahead_in, hn - hu[0], 0.0)
    coef[s, 1, lo:hi] = jnp.where(behind_in, hn + hu[0], 0.0)
    coef[s, 2, lo:hi] = jnp.where(rows < 7, hn - hu[1], 0.0)
    coef[s, 3, lo:hi] = jnp.where(rows > 0, hn + hu[1], 0.0)
    coef[s, 4, lo:hi] = jnp.where(lanes < 127, hn - hu[2], 0.0)
    coef[s, 5, lo:hi] = jnp.where(lanes > 0, hn + hu[2], 0.0)
    centre = 1.0 - 6.0 * hn
    for c in range(3):
        uc = u[c][1 : n + 1]
        slope = [
            u[c][2:] - u[c][:n],
            jnp.where(rows < 7, pltpu.roll(uc, 7, 1), 0.0)
            - jnp.where(rows > 0, pltpu.roll(uc, 1, 1), 0.0),
            jnp.where(lanes < 127, pltpu.roll(uc, 127, 2), 0.0)
            - jnp.where(lanes > 0, pltpu.roll(uc, 1, 2), 0.0),
        ]
        for d in range(3):
            local = (-0.5 * DT) * slope[d]
            if c == d:
                local = centre + local
            coef[s, 6 + 3 * c + d, lo:hi] = local


def step(s, src, dst, coef, base):
    lo, hi = span(s)
    w = [src[c, lo:hi] for c in range(3)]
    k = [coef[s, i, lo:hi] for i in range(6)]
    for c in range(3):
        new = k[0] * src[c, lo + 1 : hi + 1] + k[1] * src[c, lo - 1 : hi - 1]
        new += k[2] * pltpu.roll(w[c], 7, 1) + k[3] * pltpu.roll(w[c], 1, 1)
        new += k[4] * pltpu.roll(w[c], 127, 2) + k[5] * pltpu.roll(w[c], 1, 2)
        for d in range(3):
            new += coef[s, 6 + 3 * c + d, lo:hi] * w[d]
        dst[c, lo - base : hi - base] = new


def eliminate(gram, count):
    rows, lanes = signs((32, 128), 0), signs((32, 128), 1)
    a = jnp.where(lanes == rows + 32, 1.0, gram)
    for j in range(count):
        row = a[j : j + 1, :]
        m = jnp.where(rows > j, a[:, j : j + 1] * (1.0 / a[j : j + 1, j : j + 1]), 0.0)
        a = a - m * row
    diagonal = jnp.where(lanes == rows, a, 0.0)
    pivots = jnp.sum(diagonal, axis=1, keepdims=True)
    scale = jnp.where(rows[:, :1] < count, 1.0 / jnp.sqrt(pivots), 1.0)
    return a, diagonal, scale


def kernel(
    sizes,
    tang, flow, visc, src,
    handed, small,
    ext, mid, flowx, viscx, srcx, coef, tmp_a, tmp_b, stepped, prev,
    accs, gram, spread, part_y, part_z, part_p, logs,
    local_sems, halo_send, halo_recv, side_send, side_recv,
    shift_send, shift_recv, y_send, y_recv, z_send, z_recv, p_send, p_recv,
    log_send, log_recv, rounds,
):
    n_seg, n_space, count = sizes
    total = count + 1
    depth = n_space // ROW
    seg, pos = lax.axis_index("seg"), lax.axis_index("space")
    y, z = lax.rem(pos, ROW), pos // ROW
    right = (seg, lax.rem(pos + 1, n_space))
    left = (seg, lax.rem(pos + n_space - 1, n_space))

    def along_y(d):
        return (seg, z * ROW + lax.rem(y + d, ROW))

    def along_z(d, ds=0):
        return (lax.rem(seg + ds, n_seg), lax.rem(z + d, depth) * ROW + y)

    def along_seg(d):
        return (lax.rem(seg + d, n_seg), pos)

    near = [along_y(1), along_y(ROW - 1), along_z(1), along_z(depth - 1)]
    near += [along_seg(d % n_seg) for d in (1, -1, 2, -2)]
    greeted = [right, left] + near

    def greet(sem, devices):
        for device in devices:
            pl.semaphore_signal(sem, inc=1, device_id=device, device_id_type=MESH)

    barrier = pltpu.get_barrier_semaphore()
    greet(barrier, greeted)

    own = pl.ds(HALO, SLAB)
    locals_ = [
        pltpu.make_async_copy(tang.at[0], ext.at[:, :, own], local_sems.at[0]),
        pltpu.make_async_copy(flow.at[0], flowx.at[:, :, own], local_sems.at[1]),
        pltpu.make_async_copy(visc.at[0], viscx.at[own], local_sems.at[2]),
        pltpu.make_async_copy(src.at[0], srcx.at[:, own], local_sems.at[3]),
    ]
    for copy in locals_:
        copy.start()
    stepped[...] = jnp.zeros_like(stepped)
    gram[...] = jnp.zeros_like(gram)

    def remote(a, b, send, recv, device):
        return pltpu.make_async_remote_copy(
            src_ref=a, dst_ref=b, send_sem=send, recv_sem=recv,
            device_id=device, device_id_type=MESH,
        )

    def halo(k):
        return [
            remote(tang.at[0, k, :, pl.ds(SLAB - HALO, HALO)], ext.at[k, :, pl.ds(0, HALO)],
                   halo_send.at[0, k], halo_recv.at[0, k], right),
            remote(tang.at[0, k, :, pl.ds(0, HALO)], ext.at[k, :, pl.ds(SLAB + HALO, HALO)],
                   halo_send.at[1, k], halo_recv.at[1, k], left),
        ]

    def second(k):
        return [
            remote(mid.at[k, :, pl.ds(SLAB, HALO)], mid.at[k, :, pl.ds(0, HALO)],
                   halo_send.at[2, k], halo_recv.at[2, k], right),
            remote(mid.at[k, :, pl.ds(HALO, HALO)], mid.at[k, :, pl.ds(SLAB + HALO, HALO)],
                   halo_send.at[3, k], halo_recv.at[3, k], left),
        ]

    sides = []
    for s in range(STEPS):
        n = HALO - s % HALO
        sides.append(remote(flow.at[0, s, :, pl.ds(SLAB - n, n)], flowx.at[s, :, pl.ds(HALO - n, n)],
                            side_send.at[0, s], side_recv.at[0, s], right))
        sides.append(remote(flow.at[0, s, :, pl.ds(0, n)], flowx.at[s, :, pl.ds(SLAB + HALO, n)],
                            side_send.at[1, s], side_recv.at[1, s], left))
    n = HALO - 1
    sides.append(remote(visc.at[0, pl.ds(SLAB - n, n)], viscx.at[pl.ds(HALO - n, n)],
                        side_send.at[0, 4], side_recv.at[0, 4], right))
    sides.append(remote(visc.at[0, pl.ds(0, n)], viscx.at[pl.ds(SLAB + HALO, n)],
                        side_send.at[1, 4], side_recv.at[1, 4], left))
    sides.append(remote(src.at[0, :, pl.ds(SLAB - n, n)], srcx.at[:, pl.ds(HALO - n, n)],
                        side_send.at[0, 5], side_recv.at[0, 5], right))
    sides.append(remote(src.at[0, :, pl.ds(0, n)], srcx.at[:, pl.ds(SLAB + HALO, n)],
                        side_send.at[1, 5], side_recv.at[1, 5], left))

    pl.semaphore_wait(barrier, len(greeted))
    for copy in sides:
        copy.start()
    for k in range(min(AHEAD, total)):
        for copy in halo(k):
            copy.start()
    greet(rounds.at[0], near)
    for copy in locals_:
        copy.wait()
    for copy in sides:
        copy.wait_recv()
    for s in range(STEPS):
        coefficients(s, flowx, viscx, srcx, coef, pos, n_space * SLAB)

    def shift(k):
        return remote(stepped.at[k], prev.at[k], shift_send.at[k], shift_recv.at[k], along_seg(1))

    rows, lanes = signs((32, 128), 0), signs((32, 128), 1)

    def advance(k, s, src, dst, base):
        step(s, src, dst, coef, base)

        @pl.when(k == count)
        def _():
            lo, hi = span(s)
            for c in range(3):
                driven = dst[c, lo - base : hi - base]
                dst[c, lo - base : hi - base] = driven + DT * srcx[c, lo:hi]

    def start(k):
        for copy in halo(k):
            copy.wait_recv()

        @pl.when(k + AHEAD < total)
        def _():
            for copy in halo(k + AHEAD):
                copy.start()

        advance(k, 0, ext.at[k], tmp_a, 0)
        advance(k, 1, tmp_a, mid.at[k], 0)
        for copy in second(k):
            copy.start()

    def finish(k):
        for copy in second(k):
            copy.wait_recv()
        advance(k, 2, mid.at[k], tmp_b, 0)
        advance(k, 3, tmp_b, stepped.at[k], HALO)
        shift(k).start()
        w = stepped[k]
        for j in range(total):
            accs[8 * j : 8 * j + 8, :] = jnp.sum(w * stepped[j], axis=(0, 1))
        folded = accs[pl.ds(0, 32, stride=8), :]
        for i in range(1, 8):
            folded += accs[pl.ds(i, 32, stride=8), :]
        column = jnp.sum(folded, axis=1, keepdims=True)
        row = jnp.sum(jnp.where(rows == lanes, column, 0.0), axis=0, keepdims=True)
        g = gram[...]
        g = jnp.where((lanes == k) & (rows <= k), column, g)
        g = jnp.where((rows == k) & (lanes <= k), row, g)
        gram[...] = g

    def turn(i, carry):
        @pl.when(i == 2)
        def _():
            pl.semaphore_wait(rounds.at[0], len(near))
            greet(rounds.at[1], near[2:4])

        @pl.when(i == 4)
        def _():
            pl.semaphore_wait(rounds.at[1], 2)
            greet(rounds.at[2], near[2:4])

        @pl.when(i == 6)
        def _():
            pl.semaphore_wait(rounds.at[2], 2)
            greet(rounds.at[3], near[2:4])

        @pl.when(i == 8)
        def _():
            pl.semaphore_wait(rounds.at[3], 2)

        @pl.when(i < total)
        def _():
            start(i)

        @pl.when(i >= lag)
        def _():
            finish(i - lag)

        return carry

    lag = min(LAG, total)
    accs[8 * total :, :] = jnp.zeros((8 * (32 - total), 128), jnp.float32)
    lax.fori_loop(0, total + lag, turn, 0)

    cells = 3 * SLAB * 8 * 128 * n_space
    packed = gram[0:8, :]
    for i in range(1, 4):
        packed += pltpu.roll(gram[8 * i : 8 * i + 8, :], 32 * i, 1)
    part_y[y] = packed * (1.0 / cells)

    def exchange_y(d):
        return remote(part_y.at[y], part_y.at[y], y_send.at[d], y_recv.at[y], along_y(d))

    def exchange_z(d):
        return remote(part_z.at[z], part_z.at[z], z_send.at[d], z_recv.at[z], along_z(d))

    def exchange_p(d):
        return remote(part_z.at[z], part_p.at[z], p_send.at[d], p_recv.at[z], along_z(d, 1))

    def arrived(slot, sems, position):
        remote(slot.at[position], slot.at[position], y_send.at[0], sems.at[position], left).wait_recv()

    for d in range(1, ROW):
        exchange_y(d).start()
    for d in range(1, ROW):
        arrived(part_y, y_recv, lax.rem(y + d, ROW))
    part_z[z] = part_y[0] + part_y[1] + part_y[2] + part_y[3]
    far_first = sorted(range(depth), key=lambda d: -min(d, depth - d))
    for d in far_first[:-1]:
        exchange_z(d).start()
    for d in far_first:
        exchange_p(d).start()

    def settle(k, carry):
        for copy in halo(k) + second(k):
            copy.wait_send()
        shift(k).wait()
        return carry

    for copy in sides:
        copy.wait_send()
    lax.fori_loop(0, total, settle, 0)
    for d in range(1, ROW):
        exchange_y(d).wait_send()
    for d in range(1, depth):
        arrived(part_z, z_recv, lax.rem(z + d, depth))

    def unpack(slots):
        sums = slots[0]
        for i in range(1, depth):
            sums = sums + slots[i]
        narrow = signs((8, 128), 1) < 32
        pieces = [jnp.where(narrow, sums, 0.0)]
        for i in range(1, 4):
            pieces.append(jnp.where(narrow, pltpu.roll(sums, 128 - 32 * i, 1), 0.0))
        return jnp.concatenate(pieces, axis=0)

    mine, diagonal, scale = eliminate(unpack(part_z), count)
    lane = signs((8, 128), 1)
    pivot_row = jnp.broadcast_to(jnp.sum(diagonal, axis=0, keepdims=True), (8, 128))
    logs[seg] = 0.5 * jnp.log(jnp.where(lane < count, pivot_row, 1.0))

    def exchange_log(d):
        return remote(logs.at[seg], logs.at[seg], log_send.at[d], log_recv.at[seg], along_seg(d))

    for d in sorted(range(1, n_seg), key=lambda d: -min(d, n_seg - d)):
        exchange_log(d).start()
    for d in range(1, depth):
        exchange_z(d).wait_send()
    for d in range(depth):
        arrived(part_p, p_recv, lax.rem(z + d, depth))
    inner = jnp.where(rows == lanes, mine[:, count : count + 1] * scale, 0.0)
    small[1:2, :] = jnp.sum(inner, axis=0, keepdims=True)


    @pl.when(seg == 0)
    def _():
        def keep(k, carry):
            handed[k] = ext[k, :, HALO : HALO + SLAB]
            return carry

        lax.fori_loop(0, total, keep, 0)

    @pl.when(seg > 0)
    def _():
        before, _, before_scale = eliminate(unpack(part_p), count)
        weights = before * before_scale
        for k in range(total):
            spread[k] = jnp.broadcast_to(weights[:, 32 + k : 33 + k], (32, 128))

        def combine(i, carry):
            c, x = i // SLAB, lax.rem(i, SLAB)
            w = [prev[k, c, x] for k in range(total)]
            for j in range(total):
                new = jnp.broadcast_to(spread[0, j : j + 1, :], (8, 128)) * w[0]
                for k in range(1, j + 1):
                    new += jnp.broadcast_to(spread[k, j : j + 1, :], (8, 128)) * w[k]
                handed[j, c, x] = new
            return carry

        lax.fori_loop(0, 3 * SLAB, combine, 0)

    for d in range(1, n_seg):
        arrived(logs, log_recv, lax.rem(seg + d, n_seg))
    sums = jnp.zeros((8, 128), jnp.float32)
    for i in range(n_seg):
        sums = sums + jnp.where(i <= seg, logs[i], 0.0)
    small[0:1, :] = sums[0:1, :]

    for d in range(depth):
        exchange_p(d).wait_send()
    for d in range(1, n_seg):
        exchange_log(d).wait_send()


def body(tangents, base_flow, viscosity, source):
    n_seg, n_space = lax.axis_size("seg"), lax.axis_size("space")
    total = tangents.shape[1]
    count = total - 1
    depth = n_space // ROW
    f32 = jnp.float32
    field = (3, SLAB, 8, 128)
    dma = pltpu.SemaphoreType.DMA
    any_spec = pl.BlockSpec(memory_space=pl.ANY)
    vmem_spec = pl.BlockSpec(memory_space=pltpu.VMEM)
    inputs = [
        pltpu.with_memory_space_constraint(x, pltpu.HBM)
        for x in (tangents, base_flow, viscosity, source)
    ]
    handed, small = pl.pallas_call(
        functools.partial(kernel, (n_seg, n_space, count)),
        out_shape=(
            jax.ShapeDtypeStruct((total,) + field, f32),
            jax.ShapeDtypeStruct((8, 128), f32),
        ),
        in_specs=[any_spec] * 4,
        out_specs=(vmem_spec,) * 2,
        scratch_shapes=[
            pltpu.VMEM((total, 3, WIDE, 8, 128), f32),
            pltpu.VMEM((total, 3, WIDE, 8, 128), f32),
            pltpu.VMEM((STEPS, 3, WIDE, 8, 128), f32),
            pltpu.VMEM((WIDE, 8, 128), f32),
            pltpu.VMEM((3, WIDE, 8, 128), f32),
            pltpu.VMEM((STEPS, 15, WIDE, 8, 128), f32),
            pltpu.VMEM((3, WIDE, 8, 128), f32),
            pltpu.VMEM((3, WIDE, 8, 128), f32),
            pltpu.VMEM((total,) + field, f32),
            pltpu.VMEM((total,) + field, f32),
            pltpu.VMEM((256, 128), f32),
            pltpu.VMEM((32, 128), f32),
            pltpu.VMEM((total, 32, 128), f32),
            pltpu.VMEM((ROW, 8, 128), f32),
            pltpu.VMEM((depth, 8, 128), f32),
            pltpu.VMEM((depth, 8, 128), f32),
            pltpu.VMEM((n_seg, 8, 128), f32),
            dma((4,)),
            dma((4, total)),
            dma((4, total)),
            dma((2, 6)),
            dma((2, 6)),
            dma((total,)),
            dma((total,)),
            dma((ROW,)),
            dma((ROW,)),
            dma((depth,)),
            dma((depth,)),
            dma((depth,)),
            dma((depth,)),
            dma((n_seg,)),
            dma((n_seg,)),
            pltpu.SemaphoreType.REGULAR((4,)),
        ],
        compiler_params=pltpu.CompilerParams(
            collective_id=0, has_side_effects=True, vmem_limit_bytes=32 * 1024 * 1024
        ),
    )(*inputs)
    return (handed[None], small[0:1, :count], small[1:2, :count])


def solution(mesh):
    return jax.shard_map(
        body,
        mesh=mesh,
        in_specs=(
            P("seg", None, None, "space", None, None),
            P("seg", None, None, "space", None, None),
            P("seg", "space", None, None),
            P("seg", None, "space", None, None),
        ),
        out_specs=(P("seg", None, None, "space", None, None), P("seg", None), P("seg", None)),
        check_vma=False,
    )
```

```python
import functools

import jax
import jax.numpy as jnp
from jax import lax
from jax.experimental import pallas as pl
from jax.experimental.pallas import tpu as pltpu
from jax.sharding import PartitionSpec as P

MESH = pl.DeviceIdType.MESH
DT = 0.5
ROW = 4
SLAB = 4
HALO = 2
WIDE = SLAB + 2 * HALO
STEPS = 4
AHEAD = 12
BEHIND = 6
LAG = 12


def signs(shape, dim):
    return lax.broadcasted_iota(jnp.int32, shape, dim)


def span(s):
    edge = 1 + s % HALO
    return edge, WIDE - edge


def coefficients(s, flowx, viscx, srcx, coef, position, planes_total):
    lo, hi = span(s)
    n = hi - lo
    first = position * SLAB - HALO
    plane = first + lo - 1 + signs((n + 2, 8, 128), 0)
    inside = (plane >= 0) & (plane < planes_total)
    ahead_in, behind_in = inside[2:], inside[:n]
    rows, lanes = signs((n, 8, 128), 1), signs((n, 8, 128), 2)
    hn = DT * viscx[lo:hi]
    u = []
    for d in range(3):
        u.append(jnp.where(inside, flowx[s, d, lo - 1 : hi + 1], 0.0))
    hu = [(0.5 * DT) * u[d][1 : n + 1] for d in range(3)]
    coef[s, 0, lo:hi] = jnp.where(ahead_in, hn - hu[0], 0.0)
    coef[s, 1, lo:hi] = jnp.where(behind_in, hn + hu[0], 0.0)
    coef[s, 2, lo:hi] = jnp.where(rows < 7, hn - hu[1], 0.0)
    coef[s, 3, lo:hi] = jnp.where(rows > 0, hn + hu[1], 0.0)
    coef[s, 4, lo:hi] = jnp.where(lanes < 127, hn - hu[2], 0.0)
    coef[s, 5, lo:hi] = jnp.where(lanes > 0, hn + hu[2], 0.0)
    centre = 1.0 - 6.0 * hn
    for c in range(3):
        uc = u[c][1 : n + 1]
        slope = [
            u[c][2:] - u[c][:n],
            jnp.where(rows < 7, pltpu.roll(uc, 7, 1), 0.0)
            - jnp.where(rows > 0, pltpu.roll(uc, 1, 1), 0.0),
            jnp.where(lanes < 127, pltpu.roll(uc, 127, 2), 0.0)
            - jnp.where(lanes > 0, pltpu.roll(uc, 1, 2), 0.0),
        ]
        for d in range(3):
            local = (-0.5 * DT) * slope[d]
            if c == d:
                local = centre + local
            coef[s, 6 + 3 * c + d, lo:hi] = local


def step(s, src, dst, coef, base):
    lo, hi = span(s)
    w = [src[c, lo:hi] for c in range(3)]
    k = [coef[s, i, lo:hi] for i in range(6)]
    for c in range(3):
        new = k[0] * src[c, lo + 1 : hi + 1] + k[1] * src[c, lo - 1 : hi - 1]
        new += k[2] * pltpu.roll(w[c], 7, 1) + k[3] * pltpu.roll(w[c], 1, 1)
        new += k[4] * pltpu.roll(w[c], 127, 2) + k[5] * pltpu.roll(w[c], 1, 2)
        for d in range(3):
            new += coef[s, 6 + 3 * c + d, lo:hi] * w[d]
        dst[c, lo - base : hi - base] = new


def eliminate(gram, count):
    rows, lanes = signs((32, 128), 0), signs((32, 128), 1)
    a = jnp.where(lanes == rows + 32, 1.0, gram)
    for j in range(count):
        row = a[j : j + 1, :]
        m = jnp.where(rows > j, a[:, j : j + 1] * (1.0 / a[j : j + 1, j : j + 1]), 0.0)
        a = a - m * row
    diagonal = jnp.where(lanes == rows, a, 0.0)
    pivots = jnp.sum(diagonal, axis=1, keepdims=True)
    scale = jnp.where(rows[:, :1] < count, 1.0 / jnp.sqrt(pivots), 1.0)
    return a, diagonal, scale


def kernel(
    sizes,
    tang, flow, visc, src,
    handed, growth, proj,
    ext, mid, flowx, viscx, srcx, coef, tmp_a, tmp_b, stepped, prev,
    accs, gram, spread, part_y, part_z, part_p, logs,
    local_sems, halo_send, halo_recv, side_send, side_recv,
    shift_send, shift_recv, y_send, y_recv, z_send, z_recv, p_send, p_recv,
    log_send, log_recv, rounds,
):
    n_seg, n_space, count = sizes
    total = count + 1
    depth = n_space // ROW
    seg, pos = lax.axis_index("seg"), lax.axis_index("space")
    y, z = lax.rem(pos, ROW), pos // ROW
    right = (seg, lax.rem(pos + 1, n_space))
    left = (seg, lax.rem(pos + n_space - 1, n_space))

    def along_y(d):
        return (seg, z * ROW + lax.rem(y + d, ROW))

    def along_z(d, ds=0):
        return (lax.rem(seg + ds, n_seg), lax.rem(z + d, depth) * ROW + y)

    def along_seg(d):
        return (lax.rem(seg + d, n_seg), pos)

    near = [along_y(1), along_y(ROW - 1), along_z(1), along_z(depth - 1)]
    near += [along_seg(d % n_seg) for d in (1, -1, 2, -2)]
    greeted = [right, left] + near

    def greet(sem, devices):
        for device in devices:
            pl.semaphore_signal(sem, inc=1, device_id=device, device_id_type=MESH)

    barrier = pltpu.get_barrier_semaphore()
    greet(barrier, greeted)

    own = pl.ds(HALO, SLAB)
    locals_ = [
        pltpu.make_async_copy(tang.at[0], ext.at[:, :, own], local_sems.at[0]),
        pltpu.make_async_copy(flow.at[0], flowx.at[:, :, own], local_sems.at[1]),
        pltpu.make_async_copy(visc.at[0], viscx.at[own], local_sems.at[2]),
        pltpu.make_async_copy(src.at[0], srcx.at[:, own], local_sems.at[3]),
    ]
    for copy in locals_:
        copy.start()
    stepped[...] = jnp.zeros_like(stepped)
    gram[...] = jnp.zeros_like(gram)

    def remote(a, b, send, recv, device):
        return pltpu.make_async_remote_copy(
            src_ref=a, dst_ref=b, send_sem=send, recv_sem=recv,
            device_id=device, device_id_type=MESH,
        )

    def halo(k):
        return [
            remote(tang.at[0, k, :, pl.ds(SLAB - HALO, HALO)], ext.at[k, :, pl.ds(0, HALO)],
                   halo_send.at[0, k], halo_recv.at[0, k], right),
            remote(tang.at[0, k, :, pl.ds(0, HALO)], ext.at[k, :, pl.ds(SLAB + HALO, HALO)],
                   halo_send.at[1, k], halo_recv.at[1, k], left),
        ]

    def second(k):
        return [
            remote(mid.at[k, :, pl.ds(SLAB, HALO)], mid.at[k, :, pl.ds(0, HALO)],
                   halo_send.at[2, k], halo_recv.at[2, k], right),
            remote(mid.at[k, :, pl.ds(HALO, HALO)], mid.at[k, :, pl.ds(SLAB + HALO, HALO)],
                   halo_send.at[3, k], halo_recv.at[3, k], left),
        ]

    sides = []
    for s in range(STEPS):
        n = HALO - s % HALO
        sides.append(remote(flow.at[0, s, :, pl.ds(SLAB - n, n)], flowx.at[s, :, pl.ds(HALO - n, n)],
                            side_send.at[0, s], side_recv.at[0, s], right))
        sides.append(remote(flow.at[0, s, :, pl.ds(0, n)], flowx.at[s, :, pl.ds(SLAB + HALO, n)],
                            side_send.at[1, s], side_recv.at[1, s], left))
    n = HALO - 1
    sides.append(remote(visc.at[0, pl.ds(SLAB - n, n)], viscx.at[pl.ds(HALO - n, n)],
                        side_send.at[0, 4], side_recv.at[0, 4], right))
    sides.append(remote(visc.at[0, pl.ds(0, n)], viscx.at[pl.ds(SLAB + HALO, n)],
                        side_send.at[1, 4], side_recv.at[1, 4], left))
    sides.append(remote(src.at[0, :, pl.ds(SLAB - n, n)], srcx.at[:, pl.ds(HALO - n, n)],
                        side_send.at[0, 5], side_recv.at[0, 5], right))
    sides.append(remote(src.at[0, :, pl.ds(0, n)], srcx.at[:, pl.ds(SLAB + HALO, n)],
                        side_send.at[1, 5], side_recv.at[1, 5], left))

    pl.semaphore_wait(barrier, len(greeted))
    for copy in sides:
        copy.start()
    for k in range(min(AHEAD, total)):
        for copy in halo(k):
            copy.start()
    greet(rounds.at[0], near)
    for copy in locals_:
        copy.wait()
    for copy in sides:
        copy.wait_recv()
    for s in range(STEPS):
        coefficients(s, flowx, viscx, srcx, coef, pos, n_space * SLAB)

    def shift(k):
        return remote(stepped.at[k], prev.at[k], shift_send.at[k], shift_recv.at[k], along_seg(1))

    rows, lanes = signs((32, 128), 0), signs((32, 128), 1)

    def advance(k, s, src, dst, base):
        step(s, src, dst, coef, base)

        @pl.when(k == count)
        def _():
            lo, hi = span(s)
            for c in range(3):
                driven = dst[c, lo - base : hi - base]
                dst[c, lo - base : hi - base] = driven + DT * srcx[c, lo:hi]

    def start(k):
        for copy in halo(k):
            copy.wait_recv()

        @pl.when(k + AHEAD < total)
        def _():
            for copy in halo(k + AHEAD):
                copy.start()

        advance(k, 0, ext.at[k], tmp_a, 0)
        advance(k, 1, tmp_a, mid.at[k], 0)
        for copy in second(k):
            copy.start()

    def finish(k):
        for copy in second(k):
            copy.wait_recv()
        advance(k, 2, mid.at[k], tmp_b, 0)
        advance(k, 3, tmp_b, stepped.at[k], HALO)
        shift(k).start()
        for copy in halo(k) + second(k):
            copy.wait_send()

        @pl.when(k >= BEHIND)
        def _():
            shift(k - BEHIND).wait()

        w = stepped[k]
        for j in range(total):
            accs[8 * j : 8 * j + 8, :] = jnp.sum(w * stepped[j], axis=(0, 1))
        folded = accs[pl.ds(0, 32, stride=8), :]
        for i in range(1, 8):
            folded += accs[pl.ds(i, 32, stride=8), :]
        column = jnp.sum(folded, axis=1, keepdims=True)
        row = jnp.sum(jnp.where(rows == lanes, column, 0.0), axis=0, keepdims=True)
        g = gram[...]
        g = jnp.where((lanes == k) & (rows <= k), column, g)
        g = jnp.where((rows == k) & (lanes <= k), row, g)
        gram[...] = g

    def turn(i, carry):
        @pl.when(i == 2)
        def _():
            pl.semaphore_wait(rounds.at[0], len(near))
            greet(rounds.at[1], near[2:4])

        @pl.when(i == 4)
        def _():
            pl.semaphore_wait(rounds.at[1], 2)
            greet(rounds.at[2], near[2:4])

        @pl.when(i == 6)
        def _():
            pl.semaphore_wait(rounds.at[2], 2)
            greet(rounds.at[3], near[2:4])

        @pl.when(i == 8)
        def _():
            pl.semaphore_wait(rounds.at[3], 2)

        @pl.when(i < total)
        def _():
            start(i)

        @pl.when(i >= lag)
        def _():
            finish(i - lag)

        return carry

    lag = min(LAG, total)
    accs[8 * total :, :] = jnp.zeros((8 * (32 - total), 128), jnp.float32)
    lax.fori_loop(0, total + lag, turn, 0)

    cells = 3 * SLAB * 8 * 128 * n_space
    packed = gram[0:8, :]
    for i in range(1, 4):
        packed += pltpu.roll(gram[8 * i : 8 * i + 8, :], 32 * i, 1)
    part_y[y] = packed * (1.0 / cells)

    def exchange_y(d):
        return remote(part_y.at[y], part_y.at[y], y_send.at[d], y_recv.at[y], along_y(d))

    def exchange_z(d):
        return remote(part_z.at[z], part_z.at[z], z_send.at[d], z_recv.at[z], along_z(d))

    def exchange_p(d):
        return remote(part_z.at[z], part_p.at[z], p_send.at[d], p_recv.at[z], along_z(d, 1))

    def arrived(slot, sems, position):
        remote(slot.at[position], slot.at[position], y_send.at[0], sems.at[position], left).wait_recv()

    for d in range(1, ROW):
        exchange_y(d).start()
    for d in range(1, ROW):
        arrived(part_y, y_recv, lax.rem(y + d, ROW))
    part_z[z] = part_y[0] + part_y[1] + part_y[2] + part_y[3]
    far_first = sorted(range(depth), key=lambda d: -min(d, depth - d))
    for d in far_first[:-1]:
        exchange_z(d).start()
    for d in far_first:
        exchange_p(d).start()

    for copy in sides:
        copy.wait_send()
    for k in range(max(total - BEHIND, 0), total):
        shift(k).wait()
    for d in range(1, ROW):
        exchange_y(d).wait_send()
    for d in range(1, depth):
        arrived(part_z, z_recv, lax.rem(z + d, depth))

    def unpack(slots):
        sums = slots[0]
        for i in range(1, depth):
            sums = sums + slots[i]
        narrow = signs((8, 128), 1) < 32
        pieces = [jnp.where(narrow, sums, 0.0)]
        for i in range(1, 4):
            pieces.append(jnp.where(narrow, pltpu.roll(sums, 128 - 32 * i, 1), 0.0))
        return jnp.concatenate(pieces, axis=0)

    mine, diagonal, scale = eliminate(unpack(part_z), count)
    lane = signs((8, 128), 1)
    pivot_row = jnp.broadcast_to(jnp.sum(diagonal, axis=0, keepdims=True), (8, 128))
    logs[seg] = 0.5 * jnp.log(jnp.where(lane < count, pivot_row, 1.0))

    def exchange_log(d):
        return remote(logs.at[seg], logs.at[seg], log_send.at[d], log_recv.at[seg], along_seg(d))

    for d in sorted(range(1, n_seg), key=lambda d: -min(d, n_seg - d)):

        @pl.when(seg + d < n_seg)
        def _():
            exchange_log(d).start()

    for d in range(1, depth):
        exchange_z(d).wait_send()
    for d in range(depth):
        arrived(part_p, p_recv, lax.rem(z + d, depth))
    inner = jnp.where(rows == lanes, mine[:, count : count + 1] * scale, 0.0)
    proj[...] = jnp.sum(inner, axis=0, keepdims=True)[:, :count]


    @pl.when(seg == 0)
    def _():
        def keep(k, carry):
            handed[k] = ext[k, :, HALO : HALO + SLAB]
            return carry

        lax.fori_loop(0, total, keep, 0)

    @pl.when(seg > 0)
    def _():
        before, _, before_scale = eliminate(unpack(part_p), count)
        weights = before * before_scale
        for k in range(total):
            spread[k] = jnp.broadcast_to(weights[:, 32 + k : 33 + k], (32, 128))

        def combine(i, carry):
            c, x = i // SLAB, lax.rem(i, SLAB)
            w = [prev[k, c, x] for k in range(total)]
            for j in range(total):
                new = jnp.broadcast_to(spread[0, j : j + 1, :], (8, 128)) * w[0]
                for k in range(1, j + 1):
                    new += jnp.broadcast_to(spread[k, j : j + 1, :], (8, 128)) * w[k]
                handed[j, c, x] = new
            return carry

        lax.fori_loop(0, 3 * SLAB, combine, 0)

    for d in range(1, n_seg):

        @pl.when(seg >= d)
        def _():
            arrived(logs, log_recv, lax.rem(seg + n_seg - d, n_seg))

    sums = tmp_a.at[0, 0]
    sums[...] = logs[0]
    for i in range(1, n_seg):

        @pl.when(i <= seg)
        def _():
            sums[...] += logs[i]

    growth[...] = sums[0:1, :count]

    for d in range(depth):
        exchange_p(d).wait_send()
    for d in range(1, n_seg):

        @pl.when(seg + d < n_seg)
        def _():
            exchange_log(d).wait_send()


def deliver(handed_in, growth_in, proj_in, handed, growth, proj, sems):
    copies = [
        pltpu.make_async_copy(growth_in, growth, sems.at[0]),
        pltpu.make_async_copy(proj_in, proj, sems.at[1]),
    ]
    total = handed_in.shape[0]
    for i in range(0, total, 5):
        part = pl.ds(i, min(5, total - i))
        copies.append(pltpu.make_async_copy(handed_in.at[part], handed.at[0, part], sems.at[2 + i]))
    for copy in copies:
        copy.start()
    for copy in copies:
        copy.wait()


def body(tangents, base_flow, viscosity, source):
    n_seg, n_space = lax.axis_size("seg"), lax.axis_size("space")
    total = tangents.shape[1]
    count = total - 1
    depth = n_space // ROW
    f32 = jnp.float32
    field = (3, SLAB, 8, 128)
    dma = pltpu.SemaphoreType.DMA
    any_spec = pl.BlockSpec(memory_space=pl.ANY)
    vmem_spec = pl.BlockSpec(memory_space=pltpu.VMEM)
    inputs = [
        pltpu.with_memory_space_constraint(x, pltpu.HBM)
        for x in (tangents, base_flow, viscosity, source)
    ]
    results = pl.pallas_call(
        functools.partial(kernel, (n_seg, n_space, count)),
        out_shape=(
            jax.ShapeDtypeStruct((total,) + field, f32),
            jax.ShapeDtypeStruct((1, count), f32),
            jax.ShapeDtypeStruct((1, count), f32),
        ),
        in_specs=[any_spec] * 4,
        out_specs=(vmem_spec,) * 3,
        scratch_shapes=[
            pltpu.VMEM((total, 3, WIDE, 8, 128), f32),
            pltpu.VMEM((total, 3, WIDE, 8, 128), f32),
            pltpu.VMEM((STEPS, 3, WIDE, 8, 128), f32),
            pltpu.VMEM((WIDE, 8, 128), f32),
            pltpu.VMEM((3, WIDE, 8, 128), f32),
            pltpu.VMEM((STEPS, 15, WIDE, 8, 128), f32),
            pltpu.VMEM((3, WIDE, 8, 128), f32),
            pltpu.VMEM((3, WIDE, 8, 128), f32),
            pltpu.VMEM((total,) + field, f32),
            pltpu.VMEM((total,) + field, f32),
            pltpu.VMEM((256, 128), f32),
            pltpu.VMEM((32, 128), f32),
            pltpu.VMEM((total, 32, 128), f32),
            pltpu.VMEM((ROW, 8, 128), f32),
            pltpu.VMEM((depth, 8, 128), f32),
            pltpu.VMEM((depth, 8, 128), f32),
            pltpu.VMEM((n_seg, 8, 128), f32),
            dma((4,)),
            dma((4, total)),
            dma((4, total)),
            dma((2, 6)),
            dma((2, 6)),
            dma((total,)),
            dma((total,)),
            dma((ROW,)),
            dma((ROW,)),
            dma((depth,)),
            dma((depth,)),
            dma((depth,)),
            dma((depth,)),
            dma((n_seg,)),
            dma((n_seg,)),
            pltpu.SemaphoreType.REGULAR((4,)),
        ],
        compiler_params=pltpu.CompilerParams(
            collective_id=0, has_side_effects=True, vmem_limit_bytes=32 * 1024 * 1024
        ),
    )(*inputs)
    small = jax.ShapeDtypeStruct((1, count), f32)
    return pl.pallas_call(
        deliver,
        out_shape=(jax.ShapeDtypeStruct(tangents.shape, f32), small, small),
        in_specs=[any_spec] * 3,
        out_specs=(any_spec,) * 3,
        scratch_shapes=[dma((2 + total,))],
        compiler_params=pltpu.CompilerParams(vmem_limit_bytes=1024 * 1024),
    )(*results)


def solution(mesh):
    return jax.shard_map(
        body,
        mesh=mesh,
        in_specs=(
            P("seg", None, None, "space", None, None),
            P("seg", None, None, "space", None, None),
            P("seg", "space", None, None),
            P("seg", None, "space", None, None),
        ),
        out_specs=(P("seg", None, None, "space", None, None), P("seg", None), P("seg", None)),
        check_vma=False,
    )
```

```python
import functools

import jax
import jax.numpy as jnp
from jax import lax
from jax.experimental import pallas as pl
from jax.experimental.pallas import tpu as pltpu
from jax.sharding import PartitionSpec as P

MESH = pl.DeviceIdType.MESH
DT = 0.5
ROW = 4
SLAB = 4
HALO = 2
WIDE = SLAB + 2 * HALO
STEPS = 4
AHEAD = 12
BEHIND = 6
BLOCK = 8
LAG = 12


def signs(shape, dim):
    return lax.broadcasted_iota(jnp.int32, shape, dim)


def span(s):
    edge = 1 + s % HALO
    return edge, WIDE - edge


def coefficients(s, flowx, viscx, srcx, coef, position, planes_total):
    lo, hi = span(s)
    n = hi - lo
    first = position * SLAB - HALO
    plane = first + lo - 1 + signs((n + 2, 8, 128), 0)
    inside = (plane >= 0) & (plane < planes_total)
    ahead_in, behind_in = inside[2:], inside[:n]
    rows, lanes = signs((n, 8, 128), 1), signs((n, 8, 128), 2)
    hn = DT * viscx[lo:hi]
    u = []
    for d in range(3):
        u.append(jnp.where(inside, flowx[s, d, lo - 1 : hi + 1], 0.0))
    hu = [(0.5 * DT) * u[d][1 : n + 1] for d in range(3)]
    coef[s, 0, lo:hi] = jnp.where(ahead_in, hn - hu[0], 0.0)
    coef[s, 1, lo:hi] = jnp.where(behind_in, hn + hu[0], 0.0)
    coef[s, 2, lo:hi] = jnp.where(rows < 7, hn - hu[1], 0.0)
    coef[s, 3, lo:hi] = jnp.where(rows > 0, hn + hu[1], 0.0)
    coef[s, 4, lo:hi] = jnp.where(lanes < 127, hn - hu[2], 0.0)
    coef[s, 5, lo:hi] = jnp.where(lanes > 0, hn + hu[2], 0.0)
    centre = 1.0 - 6.0 * hn
    for c in range(3):
        uc = u[c][1 : n + 1]
        slope = [
            u[c][2:] - u[c][:n],
            jnp.where(rows < 7, pltpu.roll(uc, 7, 1), 0.0)
            - jnp.where(rows > 0, pltpu.roll(uc, 1, 1), 0.0),
            jnp.where(lanes < 127, pltpu.roll(uc, 127, 2), 0.0)
            - jnp.where(lanes > 0, pltpu.roll(uc, 1, 2), 0.0),
        ]
        for d in range(3):
            local = (-0.5 * DT) * slope[d]
            if c == d:
                local = centre + local
            coef[s, 6 + 3 * c + d, lo:hi] = local


def step(s, src, dst, coef, base):
    lo, hi = span(s)
    w = [src[c, lo:hi] for c in range(3)]
    k = [coef[s, i, lo:hi] for i in range(6)]
    for c in range(3):
        new = k[0] * src[c, lo + 1 : hi + 1] + k[1] * src[c, lo - 1 : hi - 1]
        new += k[2] * pltpu.roll(w[c], 7, 1) + k[3] * pltpu.roll(w[c], 1, 1)
        new += k[4] * pltpu.roll(w[c], 127, 2) + k[5] * pltpu.roll(w[c], 1, 2)
        for d in range(3):
            new += coef[s, 6 + 3 * c + d, lo:hi] * w[d]
        dst[c, lo - base : hi - base] = new


def eliminate(gram, count):
    rows, lanes = signs((32, 128), 0), signs((32, 128), 1)
    a = jnp.where(lanes == rows + 32, 1.0, gram)
    for first in range(0, count, BLOCK):
        pivots = range(first, min(first + BLOCK, count))
        column = {j: jnp.broadcast_to(a[:, j : j + 1], (32, 128)) for j in pivots}
        for j in pivots:
            m = jnp.where(rows > j, column[j] * (1.0 / column[j][j : j + 1, :]), 0.0)
            for later in pivots[j - first + 1 :]:
                column[later] = column[later] - m * column[later][j : j + 1, :]
            a = a - m * a[j : j + 1, :]
    diagonal = jnp.where(lanes == rows, a, 0.0)
    pivots = jnp.sum(diagonal, axis=1, keepdims=True)
    scale = jnp.where(rows[:, :1] < count, 1.0 / jnp.sqrt(pivots), 1.0)
    return a, diagonal, scale


def kernel(
    sizes,
    tang, flow, visc, src,
    handed, growth, proj,
    ext, mid, flowx, viscx, srcx, coef, tmp_a, tmp_b, stepped, prev,
    accs, gram, spread, part_y, part_z, part_p, logs,
    local_sems, halo_send, halo_recv, side_send, side_recv,
    shift_send, shift_recv, y_send, y_recv, z_send, z_recv, p_send, p_recv,
    log_send, log_recv, rounds,
):
    n_seg, n_space, count = sizes
    total = count + 1
    depth = n_space // ROW
    seg, pos = lax.axis_index("seg"), lax.axis_index("space")
    y, z = lax.rem(pos, ROW), pos // ROW
    right = (seg, lax.rem(pos + 1, n_space))
    left = (seg, lax.rem(pos + n_space - 1, n_space))

    def along_y(d):
        return (seg, z * ROW + lax.rem(y + d, ROW))

    def along_z(d, ds=0):
        return (lax.rem(seg + ds, n_seg), lax.rem(z + d, depth) * ROW + y)

    def along_seg(d):
        return (lax.rem(seg + d, n_seg), pos)

    near = [along_y(1), along_y(ROW - 1), along_z(1), along_z(depth - 1)]
    near += [along_seg(d % n_seg) for d in (1, -1, 2, -2)]
    greeted = [right, left] + near

    def greet(sem, devices):
        for device in devices:
            pl.semaphore_signal(sem, inc=1, device_id=device, device_id_type=MESH)

    barrier = pltpu.get_barrier_semaphore()
    greet(barrier, greeted)

    own = pl.ds(HALO, SLAB)
    locals_ = [
        pltpu.make_async_copy(tang.at[0], ext.at[:, :, own], local_sems.at[0]),
        pltpu.make_async_copy(flow.at[0], flowx.at[:, :, own], local_sems.at[1]),
        pltpu.make_async_copy(visc.at[0], viscx.at[own], local_sems.at[2]),
        pltpu.make_async_copy(src.at[0], srcx.at[:, own], local_sems.at[3]),
    ]
    for copy in locals_:
        copy.start()
    stepped[...] = jnp.zeros_like(stepped)
    gram[...] = jnp.zeros_like(gram)

    def remote(a, b, send, recv, device):
        return pltpu.make_async_remote_copy(
            src_ref=a, dst_ref=b, send_sem=send, recv_sem=recv,
            device_id=device, device_id_type=MESH,
        )

    def halo(k):
        return [
            remote(ext.at[k, :, pl.ds(SLAB, HALO)], ext.at[k, :, pl.ds(0, HALO)],
                   halo_send.at[0, k], halo_recv.at[0, k], right),
            remote(ext.at[k, :, pl.ds(HALO, HALO)], ext.at[k, :, pl.ds(SLAB + HALO, HALO)],
                   halo_send.at[1, k], halo_recv.at[1, k], left),
        ]

    def second(k):
        return [
            remote(mid.at[k, :, pl.ds(SLAB, HALO)], mid.at[k, :, pl.ds(0, HALO)],
                   halo_send.at[2, k], halo_recv.at[2, k], right),
            remote(mid.at[k, :, pl.ds(HALO, HALO)], mid.at[k, :, pl.ds(SLAB + HALO, HALO)],
                   halo_send.at[3, k], halo_recv.at[3, k], left),
        ]

    sides = []
    for s in range(STEPS):
        n = HALO - s % HALO
        sides.append(remote(flowx.at[s, :, pl.ds(HALO + SLAB - n, n)], flowx.at[s, :, pl.ds(HALO - n, n)],
                            side_send.at[0, s], side_recv.at[0, s], right))
        sides.append(remote(flowx.at[s, :, pl.ds(HALO, n)], flowx.at[s, :, pl.ds(SLAB + HALO, n)],
                            side_send.at[1, s], side_recv.at[1, s], left))
    n = HALO - 1
    sides.append(remote(viscx.at[pl.ds(HALO + SLAB - n, n)], viscx.at[pl.ds(HALO - n, n)],
                        side_send.at[0, 4], side_recv.at[0, 4], right))
    sides.append(remote(viscx.at[pl.ds(HALO, n)], viscx.at[pl.ds(SLAB + HALO, n)],
                        side_send.at[1, 4], side_recv.at[1, 4], left))
    sides.append(remote(srcx.at[:, pl.ds(HALO + SLAB - n, n)], srcx.at[:, pl.ds(HALO - n, n)],
                        side_send.at[0, 5], side_recv.at[0, 5], right))
    sides.append(remote(srcx.at[:, pl.ds(HALO, n)], srcx.at[:, pl.ds(SLAB + HALO, n)],
                        side_send.at[1, 5], side_recv.at[1, 5], left))

    for copy in locals_:
        copy.wait()
    pl.semaphore_wait(barrier, len(greeted))
    for copy in sides:
        copy.start()
    for k in range(min(AHEAD, total)):
        for copy in halo(k):
            copy.start()
    greet(rounds.at[0], near)
    for copy in sides:
        copy.wait_recv()
    for s in range(STEPS):
        coefficients(s, flowx, viscx, srcx, coef, pos, n_space * SLAB)

    def shift(k):
        return remote(stepped.at[k], prev.at[k], shift_send.at[k], shift_recv.at[k], along_seg(1))

    rows, lanes = signs((32, 128), 0), signs((32, 128), 1)

    def advance(k, s, src, dst, base):
        step(s, src, dst, coef, base)

        @pl.when(k == count)
        def _():
            lo, hi = span(s)
            for c in range(3):
                driven = dst[c, lo - base : hi - base]
                dst[c, lo - base : hi - base] = driven + DT * srcx[c, lo:hi]

    def start(k):
        for copy in halo(k):
            copy.wait_recv()

        @pl.when(k + AHEAD < total)
        def _():
            for copy in halo(k + AHEAD):
                copy.start()

        advance(k, 0, ext.at[k], tmp_a, 0)
        advance(k, 1, tmp_a, mid.at[k], 0)
        for copy in second(k):
            copy.start()

    def finish(k):
        for copy in second(k):
            copy.wait_recv()
        advance(k, 2, mid.at[k], tmp_b, 0)
        advance(k, 3, tmp_b, stepped.at[k], HALO)
        shift(k).start()
        for copy in halo(k) + second(k):
            copy.wait_send()

        @pl.when(k >= BEHIND)
        def _():
            shift(k - BEHIND).wait()

        w = stepped[k]
        for j in range(total):
            accs[8 * j : 8 * j + 8, :] = jnp.sum(w * stepped[j], axis=(0, 1))
        folded = accs[pl.ds(0, 32, stride=8), :]
        for i in range(1, 8):
            folded += accs[pl.ds(i, 32, stride=8), :]
        column = jnp.sum(folded, axis=1, keepdims=True)
        row = jnp.sum(jnp.where(rows == lanes, column, 0.0), axis=0, keepdims=True)
        g = gram[...]
        g = jnp.where((lanes == k) & (rows <= k), column, g)
        g = jnp.where((rows == k) & (lanes <= k), row, g)
        gram[...] = g

    def turn(i, carry):
        @pl.when(i == 2)
        def _():
            pl.semaphore_wait(rounds.at[0], len(near))
            greet(rounds.at[1], near[2:4])

        @pl.when(i == 4)
        def _():
            pl.semaphore_wait(rounds.at[1], 2)
            greet(rounds.at[2], near[2:4])

        @pl.when(i == 6)
        def _():
            pl.semaphore_wait(rounds.at[2], 2)
            greet(rounds.at[3], near[2:4])

        @pl.when(i == 8)
        def _():
            pl.semaphore_wait(rounds.at[3], 2)

        @pl.when(i < total)
        def _():
            start(i)

        @pl.when(i >= lag)
        def _():
            finish(i - lag)

        return carry

    lag = min(LAG, total)
    accs[8 * total :, :] = jnp.zeros((8 * (32 - total), 128), jnp.float32)
    lax.fori_loop(0, total + lag, turn, 0)

    cells = 3 * SLAB * 8 * 128 * n_space
    packed = gram[0:8, :]
    for i in range(1, 4):
        packed += pltpu.roll(gram[8 * i : 8 * i + 8, :], 32 * i, 1)
    part_y[y] = packed * (1.0 / cells)

    def exchange_y(d):
        return remote(part_y.at[y], part_y.at[y], y_send.at[d], y_recv.at[y], along_y(d))

    def exchange_z(d):
        return remote(part_z.at[z], part_z.at[z], z_send.at[d], z_recv.at[z], along_z(d))

    def exchange_p(d):
        return remote(part_z.at[z], part_p.at[z], p_send.at[d], p_recv.at[z], along_z(d, 1))

    def arrived(slot, sems, position):
        remote(slot.at[position], slot.at[position], y_send.at[0], sems.at[position], left).wait_recv()

    for d in range(1, ROW):
        exchange_y(d).start()
    for d in range(1, ROW):
        arrived(part_y, y_recv, lax.rem(y + d, ROW))
    part_z[z] = part_y[0] + part_y[1] + part_y[2] + part_y[3]
    far_first = sorted(range(depth), key=lambda d: -min(d, depth - d))
    for d in far_first[:-1]:
        exchange_z(d).start()
    for d in far_first:
        exchange_p(d).start()

    for copy in sides:
        copy.wait_send()
    for k in range(max(total - BEHIND, 0), total):
        shift(k).wait()
    for d in range(1, ROW):
        exchange_y(d).wait_send()
    for d in range(1, depth):
        arrived(part_z, z_recv, lax.rem(z + d, depth))

    def unpack(slots):
        sums = slots[0]
        for i in range(1, depth):
            sums = sums + slots[i]
        narrow = signs((8, 128), 1) < 32
        pieces = [jnp.where(narrow, sums, 0.0)]
        for i in range(1, 4):
            pieces.append(jnp.where(narrow, pltpu.roll(sums, 128 - 32 * i, 1), 0.0))
        return jnp.concatenate(pieces, axis=0)

    mine, diagonal, scale = eliminate(unpack(part_z), count)
    lane = signs((8, 128), 1)
    pivot_row = jnp.broadcast_to(jnp.sum(diagonal, axis=0, keepdims=True), (8, 128))
    logs[seg] = 0.5 * jnp.log(jnp.where(lane < count, pivot_row, 1.0))

    def exchange_log(d):
        return remote(logs.at[seg], logs.at[seg], log_send.at[d], log_recv.at[seg], along_seg(d))

    for d in sorted(range(1, n_seg), key=lambda d: -min(d, n_seg - d)):

        @pl.when(seg + d < n_seg)
        def _():
            exchange_log(d).start()

    for d in range(1, depth):
        exchange_z(d).wait_send()
    for d in range(depth):
        arrived(part_p, p_recv, lax.rem(z + d, depth))
    inner = jnp.where(rows == lanes, mine[:, count : count + 1] * scale, 0.0)
    proj[...] = jnp.sum(inner, axis=0, keepdims=True)[:, :count]


    @pl.when(seg == 0)
    def _():
        def keep(k, carry):
            handed[k] = ext[k, :, HALO : HALO + SLAB]
            return carry

        lax.fori_loop(0, total, keep, 0)

    @pl.when(seg > 0)
    def _():
        before, _, before_scale = eliminate(unpack(part_p), count)
        weights = before * before_scale
        for k in range(total):
            spread[k] = jnp.broadcast_to(weights[:, 32 + k : 33 + k], (32, 128))

        def combine(i, carry):
            c, x = i // SLAB, lax.rem(i, SLAB)
            w = [prev[k, c, x] for k in range(total)]
            for j in range(total):
                new = jnp.broadcast_to(spread[0, j : j + 1, :], (8, 128)) * w[0]
                for k in range(1, j + 1):
                    new += jnp.broadcast_to(spread[k, j : j + 1, :], (8, 128)) * w[k]
                handed[j, c, x] = new
            return carry

        lax.fori_loop(0, 3 * SLAB, combine, 0)

    for d in range(1, n_seg):

        @pl.when(seg >= d)
        def _():
            arrived(logs, log_recv, lax.rem(seg + n_seg - d, n_seg))

    sums = tmp_a.at[0, 0]
    sums[...] = logs[0]
    for i in range(1, n_seg):

        @pl.when(i <= seg)
        def _():
            sums[...] += logs[i]

    growth[...] = sums[0:1, :count]

    for d in range(depth):
        exchange_p(d).wait_send()
    for d in range(1, n_seg):

        @pl.when(seg + d < n_seg)
        def _():
            exchange_log(d).wait_send()


def deliver(handed_in, growth_in, proj_in, handed, growth, proj, sems):
    copies = [
        pltpu.make_async_copy(growth_in, growth, sems.at[0]),
        pltpu.make_async_copy(proj_in, proj, sems.at[1]),
    ]
    total = handed_in.shape[0]
    for i in range(0, total, 5):
        part = pl.ds(i, min(5, total - i))
        copies.append(pltpu.make_async_copy(handed_in.at[part], handed.at[0, part], sems.at[2 + i]))
    for copy in copies:
        copy.start()
    for copy in copies:
        copy.wait()


def body(tangents, base_flow, viscosity, source):
    n_seg, n_space = lax.axis_size("seg"), lax.axis_size("space")
    total = tangents.shape[1]
    count = total - 1
    depth = n_space // ROW
    f32 = jnp.float32
    field = (3, SLAB, 8, 128)
    dma = pltpu.SemaphoreType.DMA
    any_spec = pl.BlockSpec(memory_space=pl.ANY)
    vmem_spec = pl.BlockSpec(memory_space=pltpu.VMEM)
    inputs = [
        pltpu.with_memory_space_constraint(x, pltpu.HBM)
        for x in (tangents, base_flow, viscosity, source)
    ]
    results = pl.pallas_call(
        functools.partial(kernel, (n_seg, n_space, count)),
        out_shape=(
            jax.ShapeDtypeStruct((total,) + field, f32),
            jax.ShapeDtypeStruct((1, count), f32),
            jax.ShapeDtypeStruct((1, count), f32),
        ),
        in_specs=[any_spec] * 4,
        out_specs=(vmem_spec,) * 3,
        scratch_shapes=[
            pltpu.VMEM((total, 3, WIDE, 8, 128), f32),
            pltpu.VMEM((total, 3, WIDE, 8, 128), f32),
            pltpu.VMEM((STEPS, 3, WIDE, 8, 128), f32),
            pltpu.VMEM((WIDE, 8, 128), f32),
            pltpu.VMEM((3, WIDE, 8, 128), f32),
            pltpu.VMEM((STEPS, 15, WIDE, 8, 128), f32),
            pltpu.VMEM((3, WIDE, 8, 128), f32),
            pltpu.VMEM((3, WIDE, 8, 128), f32),
            pltpu.VMEM((total,) + field, f32),
            pltpu.VMEM((total,) + field, f32),
            pltpu.VMEM((256, 128), f32),
            pltpu.VMEM((32, 128), f32),
            pltpu.VMEM((total, 32, 128), f32),
            pltpu.VMEM((ROW, 8, 128), f32),
            pltpu.VMEM((depth, 8, 128), f32),
            pltpu.VMEM((depth, 8, 128), f32),
            pltpu.VMEM((n_seg, 8, 128), f32),
            dma((4,)),
            dma((4, total)),
            dma((4, total)),
            dma((2, 6)),
            dma((2, 6)),
            dma((total,)),
            dma((total,)),
            dma((ROW,)),
            dma((ROW,)),
            dma((depth,)),
            dma((depth,)),
            dma((depth,)),
            dma((depth,)),
            dma((n_seg,)),
            dma((n_seg,)),
            pltpu.SemaphoreType.REGULAR((4,)),
        ],
        compiler_params=pltpu.CompilerParams(
            collective_id=0, has_side_effects=True, vmem_limit_bytes=32 * 1024 * 1024
        ),
    )(*inputs)
    small = jax.ShapeDtypeStruct((1, count), f32)
    return pl.pallas_call(
        deliver,
        out_shape=(jax.ShapeDtypeStruct(tangents.shape, f32), small, small),
        in_specs=[any_spec] * 3,
        out_specs=(any_spec,) * 3,
        scratch_shapes=[dma((2 + total,))],
        compiler_params=pltpu.CompilerParams(vmem_limit_bytes=1024 * 1024),
    )(*results)


def solution(mesh):
    return jax.shard_map(
        body,
        mesh=mesh,
        in_specs=(
            P("seg", None, None, "space", None, None),
            P("seg", None, None, "space", None, None),
            P("seg", "space", None, None),
            P("seg", None, "space", None, None),
        ),
        out_specs=(P("seg", None, None, "space", None, None), P("seg", None), P("seg", None)),
        check_vma=False,
    )
```

```python
import functools

import jax
import jax.numpy as jnp
from jax import lax
from jax.experimental import pallas as pl
from jax.experimental.pallas import tpu as pltpu
from jax.sharding import PartitionSpec as P

MESH = pl.DeviceIdType.MESH
DT = 0.5
ROW = 4
SLAB = 4
HALO = 2
WIDE = SLAB + 2 * HALO
STEPS = 4
AHEAD = 12
BLOCK = 8
LAG = 12


def signs(shape, dim):
    return lax.broadcasted_iota(jnp.int32, shape, dim)


def span(s):
    edge = 1 + s % HALO
    return edge, WIDE - edge


def coefficients(s, flowx, viscx, srcx, coef, position, planes_total):
    lo, hi = span(s)
    n = hi - lo
    first = position * SLAB - HALO
    plane = first + lo - 1 + signs((n + 2, 8, 128), 0)
    inside = (plane >= 0) & (plane < planes_total)
    ahead_in, behind_in = inside[2:], inside[:n]
    rows, lanes = signs((n, 8, 128), 1), signs((n, 8, 128), 2)
    hn = DT * viscx[lo:hi]
    u = []
    for d in range(3):
        u.append(jnp.where(inside, flowx[s, d, lo - 1 : hi + 1], 0.0))
    hu = [(0.5 * DT) * u[d][1 : n + 1] for d in range(3)]
    coef[s, 0, lo:hi] = jnp.where(ahead_in, hn - hu[0], 0.0)
    coef[s, 1, lo:hi] = jnp.where(behind_in, hn + hu[0], 0.0)
    coef[s, 2, lo:hi] = jnp.where(rows < 7, hn - hu[1], 0.0)
    coef[s, 3, lo:hi] = jnp.where(rows > 0, hn + hu[1], 0.0)
    coef[s, 4, lo:hi] = jnp.where(lanes < 127, hn - hu[2], 0.0)
    coef[s, 5, lo:hi] = jnp.where(lanes > 0, hn + hu[2], 0.0)
    centre = 1.0 - 6.0 * hn
    for c in range(3):
        uc = u[c][1 : n + 1]
        slope = [
            u[c][2:] - u[c][:n],
            jnp.where(rows < 7, pltpu.roll(uc, 7, 1), 0.0)
            - jnp.where(rows > 0, pltpu.roll(uc, 1, 1), 0.0),
            jnp.where(lanes < 127, pltpu.roll(uc, 127, 2), 0.0)
            - jnp.where(lanes > 0, pltpu.roll(uc, 1, 2), 0.0),
        ]
        for d in range(3):
            local = (-0.5 * DT) * slope[d]
            if c == d:
                local = centre + local
            coef[s, 6 + 3 * c + d, lo:hi] = local


def step(s, src, dst, coef, base):
    lo, hi = span(s)
    w = [src[c, lo:hi] for c in range(3)]
    k = [coef[s, i, lo:hi] for i in range(6)]
    for c in range(3):
        new = k[0] * src[c, lo + 1 : hi + 1] + k[1] * src[c, lo - 1 : hi - 1]
        new += k[2] * pltpu.roll(w[c], 7, 1) + k[3] * pltpu.roll(w[c], 1, 1)
        new += k[4] * pltpu.roll(w[c], 127, 2) + k[5] * pltpu.roll(w[c], 1, 2)
        for d in range(3):
            new += coef[s, 6 + 3 * c + d, lo:hi] * w[d]
        dst[c, lo - base : hi - base] = new


def eliminate(gram, count):
    rows, lanes = signs((32, 128), 0), signs((32, 128), 1)
    a = jnp.where(lanes == rows + 32, 1.0, gram)
    for first in range(0, count, BLOCK):
        pivots = range(first, min(first + BLOCK, count))
        column = {j: jnp.broadcast_to(a[:, j : j + 1], (32, 128)) for j in pivots}
        for j in pivots:
            m = jnp.where(rows > j, column[j] * (1.0 / column[j][j : j + 1, :]), 0.0)
            for later in pivots[j - first + 1 :]:
                column[later] = column[later] - m * column[later][j : j + 1, :]
            a = a - m * a[j : j + 1, :]
    diagonal = jnp.where(lanes == rows, a, 0.0)
    pivots = jnp.sum(diagonal, axis=1, keepdims=True)
    scale = jnp.where(rows[:, :1] < count, 1.0 / jnp.sqrt(pivots), 1.0)
    return a, diagonal, scale


def kernel(
    sizes,
    tang, flow, visc, src,
    handed, growth, proj,
    ext, mid, flowx, viscx, srcx, coef, tmp_a, tmp_b, stepped, prev,
    accs, gram, spread, part_y, part_z, part_p, logs,
    local_sems, halo_send, halo_recv, side_send, side_recv,
    shift_sems, y_send, y_recv, z_send, z_recv, p_send, p_recv,
    log_send, log_recv, rounds,
):
    n_seg, n_space, count = sizes
    total = count + 1
    depth = n_space // ROW
    seg, pos = lax.axis_index("seg"), lax.axis_index("space")
    y, z = lax.rem(pos, ROW), pos // ROW
    right = (seg, lax.rem(pos + 1, n_space))
    left = (seg, lax.rem(pos + n_space - 1, n_space))

    def along_y(d):
        return (seg, z * ROW + lax.rem(y + d, ROW))

    def along_z(d, ds=0):
        return (lax.rem(seg + ds, n_seg), lax.rem(z + d, depth) * ROW + y)

    def along_seg(d):
        return (lax.rem(seg + d, n_seg), pos)

    near = [along_y(1), along_y(ROW - 1), along_z(1), along_z(depth - 1)]
    near += [along_seg(d % n_seg) for d in (1, -1, 2, -2)]
    greeted = [right, left] + near

    def greet(sem, devices):
        for device in devices:
            pl.semaphore_signal(sem, inc=1, device_id=device, device_id_type=MESH)

    barrier = pltpu.get_barrier_semaphore()
    greet(barrier, greeted)

    own = pl.ds(HALO, SLAB)
    locals_ = [
        pltpu.make_async_copy(tang.at[0], ext.at[:, :, own], local_sems.at[0]),
        pltpu.make_async_copy(flow.at[0], flowx.at[:, :, own], local_sems.at[1]),
        pltpu.make_async_copy(visc.at[0], viscx.at[own], local_sems.at[2]),
        pltpu.make_async_copy(src.at[0], srcx.at[:, own], local_sems.at[3]),
    ]
    for copy in locals_:
        copy.start()
    stepped[...] = jnp.zeros_like(stepped)
    gram[...] = jnp.zeros_like(gram)

    def remote(a, b, send, recv, device):
        return pltpu.make_async_remote_copy(
            src_ref=a, dst_ref=b, send_sem=send, recv_sem=recv,
            device_id=device, device_id_type=MESH,
        )

    def tag(k):
        return k.start if isinstance(k, pl.Slice) else k

    def halo(k):
        return [
            remote(ext.at[k, :, pl.ds(SLAB, HALO)], ext.at[k, :, pl.ds(0, HALO)],
                   halo_send.at[0], halo_recv.at[0, tag(k)], right),
            remote(ext.at[k, :, pl.ds(HALO, HALO)], ext.at[k, :, pl.ds(SLAB + HALO, HALO)],
                   halo_send.at[1], halo_recv.at[1, tag(k)], left),
        ]

    def second(k):
        return [
            remote(mid.at[k, :, pl.ds(SLAB, HALO)], mid.at[k, :, pl.ds(0, HALO)],
                   halo_send.at[2], halo_recv.at[2, tag(k)], right),
            remote(mid.at[k, :, pl.ds(HALO, HALO)], mid.at[k, :, pl.ds(SLAB + HALO, HALO)],
                   halo_send.at[3], halo_recv.at[3, tag(k)], left),
        ]

    sides = []
    for s in range(STEPS):
        n = HALO - s % HALO
        sides.append(remote(flowx.at[s, :, pl.ds(HALO + SLAB - n, n)], flowx.at[s, :, pl.ds(HALO - n, n)],
                            side_send.at[0, s], side_recv.at[0, s], right))
        sides.append(remote(flowx.at[s, :, pl.ds(HALO, n)], flowx.at[s, :, pl.ds(SLAB + HALO, n)],
                            side_send.at[1, s], side_recv.at[1, s], left))
    n = HALO - 1
    sides.append(remote(viscx.at[pl.ds(HALO + SLAB - n, n)], viscx.at[pl.ds(HALO - n, n)],
                        side_send.at[0, 4], side_recv.at[0, 4], right))
    sides.append(remote(viscx.at[pl.ds(HALO, n)], viscx.at[pl.ds(SLAB + HALO, n)],
                        side_send.at[1, 4], side_recv.at[1, 4], left))
    sides.append(remote(srcx.at[:, pl.ds(HALO + SLAB - n, n)], srcx.at[:, pl.ds(HALO - n, n)],
                        side_send.at[0, 5], side_recv.at[0, 5], right))
    sides.append(remote(srcx.at[:, pl.ds(HALO, n)], srcx.at[:, pl.ds(SLAB + HALO, n)],
                        side_send.at[1, 5], side_recv.at[1, 5], left))

    for copy in locals_:
        copy.wait()
    pl.semaphore_wait(barrier, len(greeted))
    for copy in sides:
        copy.start()
    for k in range(min(AHEAD, total)):
        for copy in halo(k):
            copy.start()
    greet(rounds.at[0], near)
    for copy in sides:
        copy.wait_recv()
    for s in range(STEPS):
        coefficients(s, flowx, viscx, srcx, coef, pos, n_space * SLAB)

    def shift(k):
        return remote(stepped.at[k], prev.at[k], shift_sems.at[0], shift_sems.at[1], along_seg(1))

    rows, lanes = signs((32, 128), 0), signs((32, 128), 1)

    def advance(k, s, src, dst, base):
        step(s, src, dst, coef, base)

        @pl.when(k == count)
        def _():
            lo, hi = span(s)
            for c in range(3):
                driven = dst[c, lo - base : hi - base]
                dst[c, lo - base : hi - base] = driven + DT * srcx[c, lo:hi]

    def start(k):
        for copy in halo(k):
            copy.wait_recv()

        @pl.when(k + AHEAD < total)
        def _():
            for copy in halo(k + AHEAD):
                copy.start()

        advance(k, 0, ext.at[k], tmp_a, 0)
        advance(k, 1, tmp_a, mid.at[k], 0)
        for copy in second(k):
            copy.start()

    def finish(k):
        for copy in second(k):
            copy.wait_recv()
        advance(k, 2, mid.at[k], tmp_b, 0)
        advance(k, 3, tmp_b, stepped.at[k], HALO)
        shift(k).start()
        w = stepped[k]
        for j in range(total):
            accs[8 * j : 8 * j + 8, :] = jnp.sum(w * stepped[j], axis=(0, 1))
        folded = accs[pl.ds(0, 32, stride=8), :]
        for i in range(1, 8):
            folded += accs[pl.ds(i, 32, stride=8), :]
        column = jnp.sum(folded, axis=1, keepdims=True)
        row = jnp.sum(jnp.where(rows == lanes, column, 0.0), axis=0, keepdims=True)
        g = gram[...]
        g = jnp.where((lanes == k) & (rows <= k), column, g)
        g = jnp.where((rows == k) & (lanes <= k), row, g)
        gram[...] = g

    def turn(i, carry):
        @pl.when(i == 2)
        def _():
            pl.semaphore_wait(rounds.at[0], len(near))
            greet(rounds.at[1], near[2:4])

        @pl.when(i == 4)
        def _():
            pl.semaphore_wait(rounds.at[1], 2)
            greet(rounds.at[2], near[2:4])

        @pl.when(i == 6)
        def _():
            pl.semaphore_wait(rounds.at[2], 2)
            greet(rounds.at[3], near[2:4])

        @pl.when(i == 8)
        def _():
            pl.semaphore_wait(rounds.at[3], 2)

        @pl.when(i < total)
        def _():
            start(i)

        @pl.when(i >= lag)
        def _():
            finish(i - lag)

        return carry

    lag = min(LAG, total)
    accs[8 * total :, :] = jnp.zeros((8 * (32 - total), 128), jnp.float32)
    lax.fori_loop(0, total + lag, turn, 0)

    cells = 3 * SLAB * 8 * 128 * n_space
    packed = gram[0:8, :]
    for i in range(1, 4):
        packed += pltpu.roll(gram[8 * i : 8 * i + 8, :], 32 * i, 1)
    part_y[y] = packed * (1.0 / cells)

    def exchange_y(d):
        return remote(part_y.at[y], part_y.at[y], y_send.at[d], y_recv.at[y], along_y(d))

    def exchange_z(d):
        return remote(part_z.at[z], part_z.at[z], z_send.at[d], z_recv.at[z], along_z(d))

    def exchange_p(d):
        return remote(part_z.at[z], part_p.at[z], p_send.at[d], p_recv.at[z], along_z(d, 1))

    def arrived(slot, sems, position):
        remote(slot.at[position], slot.at[position], y_send.at[0], sems.at[position], left).wait_recv()

    for d in range(1, ROW):
        exchange_y(d).start()
    for d in range(1, ROW):
        arrived(part_y, y_recv, lax.rem(y + d, ROW))
    part_z[z] = part_y[0] + part_y[1] + part_y[2] + part_y[3]
    far_first = sorted(range(depth), key=lambda d: -min(d, depth - d))
    for d in far_first[:-1]:
        exchange_z(d).start()
    for d in far_first:
        exchange_p(d).start()

    for copy in sides:
        copy.wait_send()
    every = pl.ds(0, total)
    for copy in halo(every) + second(every):
        copy.wait_send()
    shift(every).wait()
    for d in range(1, ROW):
        exchange_y(d).wait_send()
    for d in range(1, depth):
        arrived(part_z, z_recv, lax.rem(z + d, depth))

    def unpack(slots):
        sums = slots[0]
        for i in range(1, depth):
            sums = sums + slots[i]
        narrow = signs((8, 128), 1) < 32
        pieces = [jnp.where(narrow, sums, 0.0)]
        for i in range(1, 4):
            pieces.append(jnp.where(narrow, pltpu.roll(sums, 128 - 32 * i, 1), 0.0))
        return jnp.concatenate(pieces, axis=0)

    mine, diagonal, scale = eliminate(unpack(part_z), count)
    lane = signs((8, 128), 1)
    pivot_row = jnp.broadcast_to(jnp.sum(diagonal, axis=0, keepdims=True), (8, 128))
    logs[seg] = 0.5 * jnp.log(jnp.where(lane < count, pivot_row, 1.0))

    def exchange_log(d):
        return remote(logs.at[seg], logs.at[seg], log_send.at[d], log_recv.at[seg], along_seg(d))

    for d in sorted(range(1, n_seg), key=lambda d: -min(d, n_seg - d)):

        @pl.when(seg + d < n_seg)
        def _():
            exchange_log(d).start()

    for d in range(1, depth):
        exchange_z(d).wait_send()
    for d in range(depth):
        arrived(part_p, p_recv, lax.rem(z + d, depth))
    inner = jnp.where(rows == lanes, mine[:, count : count + 1] * scale, 0.0)
    proj[...] = jnp.sum(inner, axis=0, keepdims=True)[:, :count]


    @pl.when(seg == 0)
    def _():
        def keep(k, carry):
            handed[k] = ext[k, :, HALO : HALO + SLAB]
            return carry

        lax.fori_loop(0, total, keep, 0)

    @pl.when(seg > 0)
    def _():
        before, _, before_scale = eliminate(unpack(part_p), count)
        weights = before * before_scale
        for k in range(total):
            spread[k] = jnp.broadcast_to(weights[:, 32 + k : 33 + k], (32, 128))

        def combine(i, carry):
            c, x = i // SLAB, lax.rem(i, SLAB)
            w = [prev[k, c, x] for k in range(total)]
            for j in range(total):
                new = jnp.broadcast_to(spread[0, j : j + 1, :], (8, 128)) * w[0]
                for k in range(1, j + 1):
                    new += jnp.broadcast_to(spread[k, j : j + 1, :], (8, 128)) * w[k]
                handed[j, c, x] = new
            return carry

        lax.fori_loop(0, 3 * SLAB, combine, 0)

    for d in range(1, n_seg):

        @pl.when(seg >= d)
        def _():
            arrived(logs, log_recv, lax.rem(seg + n_seg - d, n_seg))

    sums = tmp_a.at[0, 0]
    sums[...] = logs[0]
    for i in range(1, n_seg):

        @pl.when(i <= seg)
        def _():
            sums[...] += logs[i]

    growth[...] = sums[0:1, :count]

    for d in range(depth):
        exchange_p(d).wait_send()
    for d in range(1, n_seg):

        @pl.when(seg + d < n_seg)
        def _():
            exchange_log(d).wait_send()


def deliver(handed_in, growth_in, proj_in, handed, growth, proj, sems):
    copies = [
        pltpu.make_async_copy(growth_in, growth, sems.at[0]),
        pltpu.make_async_copy(proj_in, proj, sems.at[1]),
    ]
    total = handed_in.shape[0]
    for i in range(0, total, 5):
        part = pl.ds(i, min(5, total - i))
        copies.append(pltpu.make_async_copy(handed_in.at[part], handed.at[0, part], sems.at[2 + i // 5]))
    for copy in copies:
        copy.start()
    for copy in copies:
        copy.wait()


def body(tangents, base_flow, viscosity, source):
    n_seg, n_space = lax.axis_size("seg"), lax.axis_size("space")
    total = tangents.shape[1]
    count = total - 1
    depth = n_space // ROW
    f32 = jnp.float32
    field = (3, SLAB, 8, 128)
    dma = pltpu.SemaphoreType.DMA
    any_spec = pl.BlockSpec(memory_space=pl.ANY)
    vmem_spec = pl.BlockSpec(memory_space=pltpu.VMEM)
    inputs = [
        pltpu.with_memory_space_constraint(x, pltpu.HBM)
        for x in (tangents, base_flow, viscosity, source)
    ]
    results = pl.pallas_call(
        functools.partial(kernel, (n_seg, n_space, count)),
        out_shape=(
            jax.ShapeDtypeStruct((total,) + field, f32),
            jax.ShapeDtypeStruct((1, count), f32),
            jax.ShapeDtypeStruct((1, count), f32),
        ),
        in_specs=[any_spec] * 4,
        out_specs=(vmem_spec,) * 3,
        scratch_shapes=[
            pltpu.VMEM((total, 3, WIDE, 8, 128), f32),
            pltpu.VMEM((total, 3, WIDE, 8, 128), f32),
            pltpu.VMEM((STEPS, 3, WIDE, 8, 128), f32),
            pltpu.VMEM((WIDE, 8, 128), f32),
            pltpu.VMEM((3, WIDE, 8, 128), f32),
            pltpu.VMEM((STEPS, 15, WIDE, 8, 128), f32),
            pltpu.VMEM((3, WIDE, 8, 128), f32),
            pltpu.VMEM((3, WIDE, 8, 128), f32),
            pltpu.VMEM((total,) + field, f32),
            pltpu.VMEM((total,) + field, f32),
            pltpu.VMEM((256, 128), f32),
            pltpu.VMEM((32, 128), f32),
            pltpu.VMEM((total, 32, 128), f32),
            pltpu.VMEM((ROW, 8, 128), f32),
            pltpu.VMEM((depth, 8, 128), f32),
            pltpu.VMEM((depth, 8, 128), f32),
            pltpu.VMEM((n_seg, 8, 128), f32),
            dma((4,)),
            dma((4,)),
            dma((4, total)),
            dma((2, 6)),
            dma((2, 6)),
            dma((2,)),
            dma((ROW,)),
            dma((ROW,)),
            dma((depth,)),
            dma((depth,)),
            dma((depth,)),
            dma((depth,)),
            dma((n_seg,)),
            dma((n_seg,)),
            pltpu.SemaphoreType.REGULAR((4,)),
        ],
        compiler_params=pltpu.CompilerParams(
            collective_id=0, has_side_effects=True, vmem_limit_bytes=32 * 1024 * 1024
        ),
    )(*inputs)
    small = jax.ShapeDtypeStruct((1, count), f32)
    return pl.pallas_call(
        deliver,
        out_shape=(jax.ShapeDtypeStruct(tangents.shape, f32), small, small),
        in_specs=[any_spec] * 3,
        out_specs=(any_spec,) * 3,
        scratch_shapes=[dma((2 + -(-total // 5),))],
        compiler_params=pltpu.CompilerParams(vmem_limit_bytes=1024 * 1024),
    )(*results)


def solution(mesh):
    return jax.shard_map(
        body,
        mesh=mesh,
        in_specs=(
            P("seg", None, None, "space", None, None),
            P("seg", None, None, "space", None, None),
            P("seg", "space", None, None),
            P("seg", None, "space", None, None),
        ),
        out_specs=(P("seg", None, None, "space", None, None), P("seg", None), P("seg", None)),
        check_vma=False,
    )
```

```python
import functools

import jax
import jax.numpy as jnp
from jax import lax
from jax.experimental import pallas as pl
from jax.experimental.pallas import tpu as pltpu
from jax.sharding import PartitionSpec as P

MESH = pl.DeviceIdType.MESH
DT = 0.5
ROW = 4
SLAB = 4
HALO = 2
WIDE = SLAB + 2 * HALO
STEPS = 4
AHEAD = 12
BLOCK = 8
LAG = 12


def signs(shape, dim):
    return lax.broadcasted_iota(jnp.int32, shape, dim)


def span(s):
    edge = 1 + s % HALO
    return edge, WIDE - edge


def coefficients(s, flowx, viscx, srcx, coef, position, planes_total):
    lo, hi = span(s)
    n = hi - lo
    first = position * SLAB - HALO
    plane = first + lo - 1 + signs((n + 2, 8, 128), 0)
    inside = (plane >= 0) & (plane < planes_total)
    ahead_in, behind_in = inside[2:], inside[:n]
    rows, lanes = signs((n, 8, 128), 1), signs((n, 8, 128), 2)
    hn = DT * viscx[lo:hi]
    u = []
    for d in range(3):
        u.append(jnp.where(inside, flowx[s, d, lo - 1 : hi + 1], 0.0))
    hu = [(0.5 * DT) * u[d][1 : n + 1] for d in range(3)]
    coef[s, 0, lo:hi] = jnp.where(ahead_in, hn - hu[0], 0.0)
    coef[s, 1, lo:hi] = jnp.where(behind_in, hn + hu[0], 0.0)
    coef[s, 2, lo:hi] = jnp.where(rows < 7, hn - hu[1], 0.0)
    coef[s, 3, lo:hi] = jnp.where(rows > 0, hn + hu[1], 0.0)
    coef[s, 4, lo:hi] = jnp.where(lanes < 127, hn - hu[2], 0.0)
    coef[s, 5, lo:hi] = jnp.where(lanes > 0, hn + hu[2], 0.0)
    centre = 1.0 - 6.0 * hn
    for c in range(3):
        uc = u[c][1 : n + 1]
        slope = [
            u[c][2:] - u[c][:n],
            jnp.where(rows < 7, pltpu.roll(uc, 7, 1), 0.0)
            - jnp.where(rows > 0, pltpu.roll(uc, 1, 1), 0.0),
            jnp.where(lanes < 127, pltpu.roll(uc, 127, 2), 0.0)
            - jnp.where(lanes > 0, pltpu.roll(uc, 1, 2), 0.0),
        ]
        for d in range(3):
            local = (-0.5 * DT) * slope[d]
            if c == d:
                local = centre + local
            coef[s, 6 + 3 * c + d, lo:hi] = local


def step(s, src, dst, coef, base):
    lo, hi = span(s)
    w = [src[c, lo:hi] for c in range(3)]
    k = [coef[s, i, lo:hi] for i in range(6)]
    for c in range(3):
        new = k[0] * src[c, lo + 1 : hi + 1] + k[1] * src[c, lo - 1 : hi - 1]
        new += k[2] * pltpu.roll(w[c], 7, 1) + k[3] * pltpu.roll(w[c], 1, 1)
        new += k[4] * pltpu.roll(w[c], 127, 2) + k[5] * pltpu.roll(w[c], 1, 2)
        for d in range(3):
            new += coef[s, 6 + 3 * c + d, lo:hi] * w[d]
        dst[c, lo - base : hi - base] = new


def eliminate(gram, count):
    rows, lanes = signs((32, 128), 0), signs((32, 128), 1)
    a = jnp.where(lanes == rows + 32, 1.0, gram)
    for first in range(0, count, BLOCK):
        pivots = range(first, min(first + BLOCK, count))
        column = {j: jnp.broadcast_to(a[:, j : j + 1], (32, 128)) for j in pivots}
        for j in pivots:
            m = jnp.where(rows > j, column[j] * (1.0 / column[j][j : j + 1, :]), 0.0)
            for later in pivots[j - first + 1 :]:
                column[later] = column[later] - m * column[later][j : j + 1, :]
            a = a - m * a[j : j + 1, :]
    diagonal = jnp.where(lanes == rows, a, 0.0)
    pivots = jnp.sum(diagonal, axis=1, keepdims=True)
    scale = jnp.where(rows[:, :1] < count, 1.0 / jnp.sqrt(pivots), 1.0)
    return a, diagonal, scale


def kernel(
    sizes,
    tang, flow, visc, src,
    handed, growth, proj,
    ext, mid, flowx, viscx, srcx, coef, tmp_a, tmp_b, stepped, prev,
    accs, gram, spread, part_y, part_z, part_p, logs,
    local_sems, halo_send, halo_recv, side_send, side_recv,
    shift_sems, y_sems, z_sems, p_sems,
    log_send, log_recv, rounds,
):
    n_seg, n_space, count = sizes
    total = count + 1
    depth = n_space // ROW
    seg, pos = lax.axis_index("seg"), lax.axis_index("space")
    y, z = lax.rem(pos, ROW), pos // ROW
    right = (seg, lax.rem(pos + 1, n_space))
    left = (seg, lax.rem(pos + n_space - 1, n_space))

    def along_y(d):
        return (seg, z * ROW + lax.rem(y + d, ROW))

    def along_z(d, ds=0):
        return (lax.rem(seg + ds, n_seg), lax.rem(z + d, depth) * ROW + y)

    def along_seg(d):
        return (lax.rem(seg + d, n_seg), pos)

    near = [along_y(1), along_y(ROW - 1), along_z(1), along_z(depth - 1)]
    near += [along_seg(d % n_seg) for d in (1, -1, 2, -2)]
    greeted = [right, left] + near

    def greet(sem, devices):
        for device in devices:
            pl.semaphore_signal(sem, inc=1, device_id=device, device_id_type=MESH)

    barrier = pltpu.get_barrier_semaphore()
    greet(barrier, greeted)

    own = pl.ds(HALO, SLAB)
    locals_ = [
        pltpu.make_async_copy(tang.at[0], ext.at[:, :, own], local_sems.at[0]),
        pltpu.make_async_copy(flow.at[0], flowx.at[:, :, own], local_sems.at[1]),
        pltpu.make_async_copy(visc.at[0], viscx.at[own], local_sems.at[2]),
        pltpu.make_async_copy(src.at[0], srcx.at[:, own], local_sems.at[3]),
    ]
    for copy in locals_:
        copy.start()
    stepped[...] = jnp.zeros_like(stepped)
    gram[...] = jnp.zeros_like(gram)

    def remote(a, b, send, recv, device):
        return pltpu.make_async_remote_copy(
            src_ref=a, dst_ref=b, send_sem=send, recv_sem=recv,
            device_id=device, device_id_type=MESH,
        )

    def landed(size, sem):
        remote(size, size, halo_send.at[0], sem, left).wait_recv()

    def gone(size, sem):
        remote(size, size, sem, halo_recv.at[0, 0], left).wait_send()

    def tag(k):
        return k.start if isinstance(k, pl.Slice) else k

    def halo(k):
        return [
            remote(ext.at[k, :, pl.ds(SLAB, HALO)], ext.at[k, :, pl.ds(0, HALO)],
                   halo_send.at[0], halo_recv.at[0, tag(k)], right),
            remote(ext.at[k, :, pl.ds(HALO, HALO)], ext.at[k, :, pl.ds(SLAB + HALO, HALO)],
                   halo_send.at[1], halo_recv.at[0, tag(k)], left),
        ]

    def second(k):
        return [
            remote(mid.at[k, :, pl.ds(SLAB, HALO)], mid.at[k, :, pl.ds(0, HALO)],
                   halo_send.at[2], halo_recv.at[1, tag(k)], right),
            remote(mid.at[k, :, pl.ds(HALO, HALO)], mid.at[k, :, pl.ds(SLAB + HALO, HALO)],
                   halo_send.at[3], halo_recv.at[1, tag(k)], left),
        ]

    sides = []
    for s in range(STEPS):
        n = HALO - s % HALO
        sides.append(remote(flowx.at[s, :, pl.ds(HALO + SLAB - n, n)], flowx.at[s, :, pl.ds(HALO - n, n)],
                            side_send.at[0, s], side_recv.at[0, s], right))
        sides.append(remote(flowx.at[s, :, pl.ds(HALO, n)], flowx.at[s, :, pl.ds(SLAB + HALO, n)],
                            side_send.at[1, s], side_recv.at[1, s], left))
    n = HALO - 1
    sides.append(remote(viscx.at[pl.ds(HALO + SLAB - n, n)], viscx.at[pl.ds(HALO - n, n)],
                        side_send.at[0, 4], side_recv.at[0, 4], right))
    sides.append(remote(viscx.at[pl.ds(HALO, n)], viscx.at[pl.ds(SLAB + HALO, n)],
                        side_send.at[1, 4], side_recv.at[1, 4], left))
    sides.append(remote(srcx.at[:, pl.ds(HALO + SLAB - n, n)], srcx.at[:, pl.ds(HALO - n, n)],
                        side_send.at[0, 5], side_recv.at[0, 5], right))
    sides.append(remote(srcx.at[:, pl.ds(HALO, n)], srcx.at[:, pl.ds(SLAB + HALO, n)],
                        side_send.at[1, 5], side_recv.at[1, 5], left))

    for copy in locals_:
        copy.wait()
    pl.semaphore_wait(barrier, len(greeted))
    for copy in sides:
        copy.start()
    for k in range(min(AHEAD, total)):
        for copy in halo(k):
            copy.start()
    greet(rounds.at[0], near)
    for copy in sides:
        copy.wait_recv()
    for s in range(STEPS):
        coefficients(s, flowx, viscx, srcx, coef, pos, n_space * SLAB)

    def shift(k):
        return remote(stepped.at[k], prev.at[k], shift_sems.at[0], shift_sems.at[1], along_seg(1))

    rows, lanes = signs((32, 128), 0), signs((32, 128), 1)

    def advance(k, s, src, dst, base):
        step(s, src, dst, coef, base)

        @pl.when(k == count)
        def _():
            lo, hi = span(s)
            for c in range(3):
                driven = dst[c, lo - base : hi - base]
                dst[c, lo - base : hi - base] = driven + DT * srcx[c, lo:hi]

    def start(k):
        landed(ext.at[k, :, pl.ds(0, 2 * HALO)], halo_recv.at[0, k])

        @pl.when(k + AHEAD < total)
        def _():
            for copy in halo(k + AHEAD):
                copy.start()

        advance(k, 0, ext.at[k], tmp_a, 0)
        advance(k, 1, tmp_a, mid.at[k], 0)
        for copy in second(k):
            copy.start()

    def finish(k):
        landed(mid.at[k, :, pl.ds(0, 2 * HALO)], halo_recv.at[1, k])
        advance(k, 2, mid.at[k], tmp_b, 0)
        advance(k, 3, tmp_b, stepped.at[k], HALO)
        shift(k).start()
        w = stepped[k]
        for j in range(total):
            accs[8 * j : 8 * j + 8, :] = jnp.sum(w * stepped[j], axis=(0, 1))
        folded = accs[pl.ds(0, 32, stride=8), :]
        for i in range(1, 8):
            folded += accs[pl.ds(i, 32, stride=8), :]
        column = jnp.sum(folded, axis=1, keepdims=True)
        row = jnp.sum(jnp.where(rows == lanes, column, 0.0), axis=0, keepdims=True)
        g = gram[...]
        g = jnp.where((lanes == k) & (rows <= k), column, g)
        g = jnp.where((rows == k) & (lanes <= k), row, g)
        gram[...] = g

    def turn(i, carry):
        @pl.when(i == 2)
        def _():
            pl.semaphore_wait(rounds.at[0], len(near))
            greet(rounds.at[1], near[2:4])

        @pl.when(i == 4)
        def _():
            pl.semaphore_wait(rounds.at[1], 2)
            greet(rounds.at[2], near[2:4])

        @pl.when(i == 6)
        def _():
            pl.semaphore_wait(rounds.at[2], 2)
            greet(rounds.at[3], near[2:4])

        @pl.when(i == 8)
        def _():
            pl.semaphore_wait(rounds.at[3], 2)

        @pl.when(i < total)
        def _():
            start(i)

        @pl.when(i >= lag)
        def _():
            finish(i - lag)

        return carry

    lag = min(LAG, total)
    accs[8 * total :, :] = jnp.zeros((8 * (32 - total), 128), jnp.float32)
    lax.fori_loop(0, total + lag, turn, 0)

    cells = 3 * SLAB * 8 * 128 * n_space
    packed = gram[0:8, :]
    for i in range(1, 4):
        packed += pltpu.roll(gram[8 * i : 8 * i + 8, :], 32 * i, 1)
    part_y[y] = packed * (1.0 / cells)

    def exchange_y(d):
        return remote(part_y.at[y], part_y.at[y], y_sems.at[0], y_sems.at[1], along_y(d))

    def exchange_z(d):
        return remote(part_z.at[z], part_z.at[z], z_sems.at[0], z_sems.at[1], along_z(d))

    def exchange_p(d):
        return remote(part_z.at[z], part_p.at[z], p_sems.at[0], p_sems.at[1], along_z(d, 1))

    def arrived(slot, sems, position):
        remote(slot.at[position], slot.at[position], y_sems.at[0], sems.at[position], left).wait_recv()

    for d in range(1, ROW):
        exchange_y(d).start()
    landed(part_y.at[pl.ds(0, ROW - 1)], y_sems.at[1])
    part_z[z] = part_y[0] + part_y[1] + part_y[2] + part_y[3]
    far_first = sorted(range(depth), key=lambda d: -min(d, depth - d))
    for d in far_first[:-1]:
        exchange_z(d).start()
    for d in far_first:
        exchange_p(d).start()

    for copy in sides:
        copy.wait_send()
    every = pl.ds(0, total)
    for copy in halo(every) + second(every):
        copy.wait_send()
    shift(every).wait()
    gone(part_y.at[pl.ds(0, ROW - 1)], y_sems.at[0])
    landed(part_z.at[pl.ds(0, depth - 1)], z_sems.at[1])

    def unpack(slots):
        sums = slots[0]
        for i in range(1, depth):
            sums = sums + slots[i]
        narrow = signs((8, 128), 1) < 32
        pieces = [jnp.where(narrow, sums, 0.0)]
        for i in range(1, 4):
            pieces.append(jnp.where(narrow, pltpu.roll(sums, 128 - 32 * i, 1), 0.0))
        return jnp.concatenate(pieces, axis=0)

    mine, diagonal, scale = eliminate(unpack(part_z), count)
    lane = signs((8, 128), 1)
    pivot_row = jnp.broadcast_to(jnp.sum(diagonal, axis=0, keepdims=True), (8, 128))
    logs[seg] = 0.5 * jnp.log(jnp.where(lane < count, pivot_row, 1.0))

    def exchange_log(d):
        return remote(logs.at[seg], logs.at[seg], log_send.at[d], log_recv.at[seg], along_seg(d))

    for d in sorted(range(1, n_seg), key=lambda d: -min(d, n_seg - d)):

        @pl.when(seg + d < n_seg)
        def _():
            exchange_log(d).start()

    gone(part_z.at[pl.ds(0, depth - 1)], z_sems.at[0])
    landed(part_p, p_sems.at[1])
    inner = jnp.where(rows == lanes, mine[:, count : count + 1] * scale, 0.0)
    proj[...] = jnp.sum(inner, axis=0, keepdims=True)[:, :count]


    @pl.when(seg == 0)
    def _():
        def keep(k, carry):
            handed[k] = ext[k, :, HALO : HALO + SLAB]
            return carry

        lax.fori_loop(0, total, keep, 0)

    @pl.when(seg > 0)
    def _():
        before, _, before_scale = eliminate(unpack(part_p), count)
        weights = before * before_scale
        for k in range(total):
            spread[k] = jnp.broadcast_to(weights[:, 32 + k : 33 + k], (32, 128))

        def combine(i, carry):
            c, x = i // SLAB, lax.rem(i, SLAB)
            w = [prev[k, c, x] for k in range(total)]
            for j in range(total):
                new = jnp.broadcast_to(spread[0, j : j + 1, :], (8, 128)) * w[0]
                for k in range(1, j + 1):
                    new += jnp.broadcast_to(spread[k, j : j + 1, :], (8, 128)) * w[k]
                handed[j, c, x] = new
            return carry

        lax.fori_loop(0, 3 * SLAB, combine, 0)

    for d in range(1, n_seg):

        @pl.when(seg >= d)
        def _():
            arrived(logs, log_recv, lax.rem(seg + n_seg - d, n_seg))

    sums = tmp_a.at[0, 0]
    sums[...] = logs[0]
    for i in range(1, n_seg):

        @pl.when(i <= seg)
        def _():
            sums[...] += logs[i]

    growth[...] = sums[0:1, :count]

    gone(part_p, p_sems.at[0])
    for d in range(1, n_seg):

        @pl.when(seg + d < n_seg)
        def _():
            exchange_log(d).wait_send()


def deliver(handed_in, growth_in, proj_in, handed, growth, proj, sems):
    copies = [
        pltpu.make_async_copy(growth_in, growth, sems.at[0]),
        pltpu.make_async_copy(proj_in, proj, sems.at[1]),
    ]
    total = handed_in.shape[0]
    for i in range(0, total, 5):
        part = pl.ds(i, min(5, total - i))
        copies.append(pltpu.make_async_copy(handed_in.at[part], handed.at[0, part], sems.at[2 + i // 5]))
    for copy in copies:
        copy.start()
    for copy in copies:
        copy.wait()


def body(tangents, base_flow, viscosity, source):
    n_seg, n_space = lax.axis_size("seg"), lax.axis_size("space")
    total = tangents.shape[1]
    count = total - 1
    depth = n_space // ROW
    f32 = jnp.float32
    field = (3, SLAB, 8, 128)
    dma = pltpu.SemaphoreType.DMA
    any_spec = pl.BlockSpec(memory_space=pl.ANY)
    vmem_spec = pl.BlockSpec(memory_space=pltpu.VMEM)
    inputs = [
        pltpu.with_memory_space_constraint(x, pltpu.HBM)
        for x in (tangents, base_flow, viscosity, source)
    ]
    results = pl.pallas_call(
        functools.partial(kernel, (n_seg, n_space, count)),
        out_shape=(
            jax.ShapeDtypeStruct((total,) + field, f32),
            jax.ShapeDtypeStruct((1, count), f32),
            jax.ShapeDtypeStruct((1, count), f32),
        ),
        in_specs=[any_spec] * 4,
        out_specs=(vmem_spec,) * 3,
        scratch_shapes=[
            pltpu.VMEM((total, 3, WIDE, 8, 128), f32),
            pltpu.VMEM((total, 3, WIDE, 8, 128), f32),
            pltpu.VMEM((STEPS, 3, WIDE, 8, 128), f32),
            pltpu.VMEM((WIDE, 8, 128), f32),
            pltpu.VMEM((3, WIDE, 8, 128), f32),
            pltpu.VMEM((STEPS, 15, WIDE, 8, 128), f32),
            pltpu.VMEM((3, WIDE, 8, 128), f32),
            pltpu.VMEM((3, WIDE, 8, 128), f32),
            pltpu.VMEM((total,) + field, f32),
            pltpu.VMEM((total,) + field, f32),
            pltpu.VMEM((256, 128), f32),
            pltpu.VMEM((32, 128), f32),
            pltpu.VMEM((total, 32, 128), f32),
            pltpu.VMEM((ROW, 8, 128), f32),
            pltpu.VMEM((depth, 8, 128), f32),
            pltpu.VMEM((depth, 8, 128), f32),
            pltpu.VMEM((n_seg, 8, 128), f32),
            dma((4,)),
            dma((4,)),
            dma((2, total)),
            dma((2, 6)),
            dma((2, 6)),
            dma((2,)),
            dma((2,)),
            dma((2,)),
            dma((2,)),
            dma((n_seg,)),
            dma((n_seg,)),
            pltpu.SemaphoreType.REGULAR((4,)),
        ],
        compiler_params=pltpu.CompilerParams(
            collective_id=0, has_side_effects=True, vmem_limit_bytes=32 * 1024 * 1024
        ),
    )(*inputs)
    small = jax.ShapeDtypeStruct((1, count), f32)
    return pl.pallas_call(
        deliver,
        out_shape=(jax.ShapeDtypeStruct(tangents.shape, f32), small, small),
        in_specs=[any_spec] * 3,
        out_specs=(any_spec,) * 3,
        scratch_shapes=[dma((2 + -(-total // 5),))],
        compiler_params=pltpu.CompilerParams(vmem_limit_bytes=1024 * 1024),
    )(*results)


def solution(mesh):
    return jax.shard_map(
        body,
        mesh=mesh,
        in_specs=(
            P("seg", None, None, "space", None, None),
            P("seg", None, None, "space", None, None),
            P("seg", "space", None, None),
            P("seg", None, "space", None, None),
        ),
        out_specs=(P("seg", None, None, "space", None, None), P("seg", None), P("seg", None)),
        check_vma=False,
    )
```
